32 devices in a mesh: seq: 2 (over x), dp: 16 (over z, y, core).
Axes of the slice: x: 2, y: 2, z: 4, core: 2. Of those that a mesh axis runs over, the one named last changes fastest.
Arguments:
- tokens: bfloat16 [16, 1536, 1024], P('dp', 'seq'), may hold values from -6 to 6
- domain: int32 [16], P('dp'), may hold values from 0 to 7
- domain_table: bfloat16 [8, 1024], replicated, may hold values from -3 to 3
- gain_one: bfloat16 [1024], replicated, may hold values from 0.25 to 1.75
- shift_one: bfloat16 [1024], replicated, may hold values from -1.5 to 1.5
- query_key_value_weight: bfloat16 [1024, 3072], replicated, may hold values from -0.1875 to 0.1875
- bias_q: bfloat16 [1024], replicated, may hold values from -1.5 to 1.5
- bias_v: bfloat16 [1024], replicated, may hold values from -1.5 to 1.5
- attention_output_weight: bfloat16 [1024, 1024], replicated, may hold values from -0.5 to 0.5
- attention_output_bias: bfloat16 [1024], replicated, may hold values from -1.5 to 1.5
- gain_two: bfloat16 [1024], replicated, may hold values from 0.25 to 1.75
- shift_two: bfloat16 [1024], replicated, may hold values from -1.5 to 1.5
- up_weight: bfloat16 [1024, 2048], replicated, may hold values from -0.1875 to 0.1875
- up_projection_bias: bfloat16 [2048], replicated, may hold values from -1.5 to 1.5
- down_weight: bfloat16 [2048, 1024], replicated, may hold values from -0.125 to 0.125
- down_projection_bias: bfloat16 [1024], replicated, may hold values from -1.5 to 1.5
- cotangent: bfloat16 [16, 1536, 1024], P('dp', 'seq'), may hold values from -6 to 6
Outputs:
- output: bfloat16 [16, 1536, 1024], P('dp', 'seq')
- grad_tokens: bfloat16 [16, 1536, 1024], P('dp', 'seq')
- grad_domain_table: float32 [8, 1024], P(None, ('seq', 'dp'))
- grad_gain_one: float32 [1024], P(('seq', 'dp'))
- grad_shift_one: float32 [1024], P(('seq', 'dp'))
- grad_w_qkv: float32 [1024, 3072], P(('seq', 'dp'))
- grad_bias_q: float32 [1024], P(('seq', 'dp'))
- grad_bias_v: float32 [1024], P(('seq', 'dp'))
- grad_w_out: float32 [1024, 1024], P(('seq', 'dp'))
- grad_bias_out: float32 [1024], P(('seq', 'dp'))
- grad_gain_two: float32 [1024], P(('seq', 'dp'))
- grad_shift_two: float32 [1024], P(('seq', 'dp'))
- grad_w_up: float32 [1024, 2048], P(('seq', 'dp'))
- grad_bias_up: float32 [2048], P(('seq', 'dp'))
- grad_w_down: float32 [2048, 1024], P(('seq', 'dp'))
- grad_bias_down: float32 [1024], P(('seq', 'dp'))
The draws below stay inside these ranges and needn't reach their ends.
All inputs are finite; a program needn't handle non-finite values.
Results may differ from the reference program's by a relative error of at most 0.014.
Values may be sent and summed in bfloat16 or wider, within the bound.
No kernel may reach another device: no remote copies, remote signals or barrier semaphores. Data moves between devices by JAX's collectives and lax.ppermute only.
A program may use at most 256 MiB of HBM per device.

```python
import math
import jax
import jax.numpy as jnp
import numpy as np
from jax import lax

D = 1024
HEAD_DIM = 128
FF = 2048
DOMAINS = 8
LENGTH = 1536
SERIES = 16


def place_ends(entries, key, least, top_value):
    extent = entries.shape
    spot = [jax.random.randint(jax.random.fold_in(key, axis), (), 0, extent[axis]) for axis in range(len(extent))]
    entries = entries.at[tuple(spot)].set(least)
    longest = extent.index(max(extent))
    spot[longest] = (spot[longest] + 1) % extent[longest]
    return entries.at[tuple(spot)].set(top_value)


def block_scale(own_key, dims, shards, low, top_value):
    def one(axis_at, shards_of):
        steps = jax.random.uniform(jax.random.fold_in(jax.random.fold_in(own_key, 6), axis_at), (shards_of,), jnp.float32, low / len(shards), top_value / len(shards))
        return jnp.repeat(jnp.exp(steps), dims[axis_at] // shards_of).reshape((-1,) + (1,) * (len(dims) - axis_at - 1))

    gain = one(*shards[0])
    for cut in shards[1:]:
        gain = gain * one(*cut)
    return gain


def rank_bounds(number_of, lean):
    weights = [(1 << 20) // math.isqrt(standing ** lean) + 1 for standing in range(1, number_of + 1)]
    deviation = 1 + sum(weights) // (1 << 30)
    return np.cumsum(np.array([max(1, weight // deviation) for weight in weights]))


def skewed_ids(key, shape, amount, lean):
    table = rank_bounds(amount, lean)
    lot = jax.random.randint(jax.random.fold_in(key, 1), shape, 0, int(table[amount - 1]))
    standing = jnp.searchsorted(jnp.asarray(table, jnp.int32), lot, side="right")
    return jax.random.permutation(jax.random.fold_in(key, 2), amount)[standing].astype(jnp.int32)


def centred(key, shape, scale, limit, shards=(), kind=jnp.bfloat16):
    array = jax.random.normal(key, shape, jnp.float32) * scale
    if len(shards) > 0:
        array = block_scale(key, shape, shards, -0.22, 0.18) * array
    return jnp.clip(array, min=-limit, max=limit).astype(kind)


def setup_inputs(seed: int = 0) -> dict:
    key_of = jax.random.split(jax.random.key(seed), 18)
    return {
        "tokens": centred(key_of[0], (SERIES, LENGTH, D), 1.0, 6.0, ((0, 16), (1, 2))),
        "domain": place_ends(skewed_ids(key_of[1], (SERIES,), DOMAINS, 2), jax.random.fold_in(key_of[1], 3), 0, DOMAINS - 1).astype(jnp.int32),
        "domain_table": centred(key_of[2], (DOMAINS, D), 0.5, 3.0),
        "gain_one": jnp.clip(1.0 + 0.15 * jax.random.normal(key_of[3], (D,), jnp.float32), 0.25, 1.75).astype(jnp.bfloat16),
        "shift_one": centred(key_of[4], (D,), 0.3, 1.5),
        "query_key_value_weight": centred(key_of[5], (D, 3 * D), D ** -0.5, 0.1875),
        "bias_q": centred(key_of[6], (D,), 0.3, 1.5),
        "bias_v": centred(key_of[7], (D,), 0.3, 1.5),
        "attention_output_weight": centred(key_of[8], (D, D), (D // 8) ** -0.5, 0.5),
        "attention_output_bias": centred(key_of[9], (D,), 0.3, 1.5),
        "gain_two": jnp.clip(1.0 + 0.15 * jax.random.normal(key_of[10], (D,), jnp.float32), 0.25, 1.75).astype(jnp.bfloat16),
        "shift_two": centred(key_of[11], (D,), 0.3, 1.5),
        "up_weight": centred(key_of[12], (D, FF), D ** -0.5, 0.1875),
        "up_projection_bias": centred(key_of[13], (FF,), 0.3, 1.5),
        "down_weight": centred(key_of[14], (FF, D), FF ** -0.5, 0.125),
        "down_projection_bias": centred(key_of[15], (D,), 0.3, 1.5),
        "cotangent": centred(key_of[16], (SERIES, LENGTH, D), 1.0, 6.0, ((0, 16), (1, 2))),
    }


@jax.custom_vjp
def low(v):
    return lax.optimization_barrier(v.astype(jnp.bfloat16)).astype(jnp.float32)

@jax.custom_vjp
def reduced_backward(v):
    return v

def low_keep(v):
    return (low(v), None)

def low_pass(kept, grad):
    return (grad,)

def back_keep(v):
    return (v, None)

def back_low(kept, grad):
    return (low(grad),)
low.defvjp(low_keep, low_pass)
reduced_backward.defvjp(back_keep, back_low)
epsilon = 1e-05
masked_score = -1e+30

def highest_precision(pattern, first_operand, second_operand):
    return jnp.einsum(pattern, first_operand, second_operand, precision=lax.Precision.HIGHEST)

def both_ways(values):
    return low(reduced_backward(values))

def layer_norm(inputs, gain_row, offset):
    center = inputs - lax.optimization_barrier(jnp.mean(inputs, axis=-1, keepdims=True))
    spread = lax.optimization_barrier(jnp.mean(center * center, axis=-1, keepdims=True))
    return center * lax.rsqrt(spread + epsilon) * gain_row + offset

def forward(params, inputs, onehot):
    domain_table, gain_one, shift_one, query_key_value_weight, bias_q, bias_v, attention_output_weight, attention_output_bias, gain_two, shift_two, up_weight, up_projection_bias, down_weight, down_projection_bias = params
    series_count, context, model_width = inputs.shape
    head_count = model_width // HEAD_DIM
    head_shape = (series_count, context, head_count, HEAD_DIM)
    embedded = inputs + highest_precision('sm,md->sd', onehot, domain_table)[:, None, :]
    first_normalized = low(layer_norm(embedded, gain_one, shift_one))
    merged_heads = highest_precision('jbk,ku->jbu', first_normalized, query_key_value_weight)
    queries = both_ways(merged_heads[..., :model_width] + bias_q).reshape(head_shape)
    key_heads = both_ways(merged_heads[..., model_width:2 * model_width]).reshape(head_shape)
    value_heads = both_ways(merged_heads[..., 2 * model_width:] + bias_v).reshape(head_shape)
    scores = reduced_backward(highest_precision('sqhe,skhe->shqk', queries, key_heads) * HEAD_DIM ** (-0.5))
    causal = jnp.tril(jnp.ones((context, context), dtype=bool))
    scores = jnp.where(causal, scores, masked_score)
    exponent = jnp.exp(scores - lax.optimization_barrier(jnp.max(scores, axis=-1, keepdims=True)))
    soft_weights = exponent / lax.optimization_barrier(jnp.sum(exponent, axis=-1, keepdims=True))
    attention_result = both_ways(highest_precision('shqk,skhe->sqhe', low(soft_weights), value_heads))
    attention_result = attention_result.reshape(series_count, context, model_width)
    residual_branch = reduced_backward(highest_precision('jbk,ku->jbu', attention_result, attention_output_weight) + attention_output_bias)
    middle = embedded + residual_branch
    second_normalized = low(layer_norm(middle, gain_two, shift_two))
    up_projected = reduced_backward(highest_precision('kmy,yv->kmv', second_normalized, up_weight) + up_projection_bias)
    activated_hidden = low(jax.nn.gelu(up_projected, approximate=False))
    reduced_copy = reduced_backward(highest_precision('qge,ek->qgk', activated_hidden, down_weight) + down_projection_bias)
    return middle + reduced_copy

def reference(tokens, domain, domain_table, gain_one, shift_one, query_key_value_weight, bias_q, bias_v, attention_output_weight, attention_output_bias, gain_two, shift_two, up_weight, up_projection_bias, down_weight, down_projection_bias, cotangent):
    params = tuple((argument.astype(jnp.float32) for argument in (domain_table, gain_one, shift_one, query_key_value_weight, bias_q, bias_v, attention_output_weight, attention_output_bias, gain_two, shift_two, up_weight, up_projection_bias, down_weight, down_projection_bias)))
    group_size = 2
    groups = SERIES // group_size
    inputs = tokens.astype(jnp.float32).reshape(groups, group_size, LENGTH, D)
    cotans = cotangent.astype(jnp.float32).reshape(groups, group_size, LENGTH, D)
    onehot = (domain[:, None] == jnp.arange(DOMAINS, dtype=jnp.int32)[None, :]).astype(jnp.float32)
    onehot = onehot.reshape(groups, group_size, DOMAINS)

    def one_group(totals, pieces):
        group_in, group_cot, group_hot = pieces
        result, pullback = jax.vjp(lambda weights, activations: forward(weights, activations, group_hot), params, group_in)
        weight_grads, input_grad = pullback(group_cot)
        totals = jax.tree.map(lambda first_value, second_value: first_value + second_value, totals, weight_grads)
        return (totals, (result.astype(jnp.bfloat16), input_grad.astype(jnp.bfloat16)))
    zero_grads = tuple((jnp.zeros_like(argument) for argument in params))
    totals, (outputs, input_grads) = lax.scan(one_group, zero_grads, (inputs, cotans, onehot))
    return (outputs.reshape(SERIES, LENGTH, D), input_grads.reshape(SERIES, LENGTH, D), totals[0], totals[1], totals[2], totals[3], totals[4], totals[5], totals[6], totals[7], totals[8], totals[9], totals[10], totals[11], totals[12], totals[13])
```

```python
import functools

import jax
import jax.numpy as jnp
from jax import lax
from jax.experimental import pallas as pl
from jax.experimental.pallas import tpu as pltpu
from jax.sharding import PartitionSpec as P

HEAD_DIM = 128
EPSILON = 1e-05
LOG2E = 1.4426950408889634
BLOCK = 256
f32, bf16 = jnp.float32, jnp.bfloat16
NN = ((1,), (0,))
NT = ((1,), (1,))
TN = ((0,), (0,))
SMEM = pl.BlockSpec(memory_space=pltpu.SMEM)


def dot(a, b, dims):
    return lax.dot_general(a, b, (dims, ((), ())), preferred_element_type=f32)


def call(kernel, grid, in_specs, out_specs, out_shape, flops, moved, scratch=(), mib=56, aliases=None):
    return pl.pallas_call(
        kernel,
        grid=grid,
        in_specs=in_specs,
        out_specs=out_specs,
        out_shape=out_shape,
        scratch_shapes=list(scratch),
        input_output_aliases=aliases or {},
        cost_estimate=pl.CostEstimate(flops=int(flops), bytes_accessed=int(moved), transcendentals=0),
        compiler_params=pltpu.CompilerParams(vmem_limit_bytes=mib * 2**20),
    )


def shape(dims, kind):
    return jax.ShapeDtypeStruct(dims, kind)


def whole(*dims):
    return pl.BlockSpec(dims, lambda *_: (0,) * len(dims), pipeline_mode=pl.Buffered(1))


def held(*dims):
    return pl.BlockSpec(dims, lambda *_: (0,) * len(dims))


def ln_parts(x):
    center = x - jnp.mean(x, axis=-1, keepdims=True)
    rstd = lax.rsqrt(jnp.mean(center * center, axis=-1, keepdims=True) + EPSILON)
    return center * rstd, rstd


def ln_back(grad, hat, rstd, gain):
    g = grad * gain
    return rstd * (g - jnp.mean(g, axis=-1, keepdims=True) - hat * jnp.mean(g * hat, axis=-1, keepdims=True))


def col_sum(a):
    return jnp.sum(a.astype(f32), axis=0, keepdims=True)


def project_kernel(x_ref, row_ref, gain_ref, shift_ref, w_ref, bias_ref, normed_ref, out_ref):
    @pl.when(pl.program_id(0) == 0)
    def _():
        for i in range(x_ref.shape[0] // BLOCK):
            rows = slice(i * BLOCK, (i + 1) * BLOCK)
            hat, _ = ln_parts(x_ref[rows, :].astype(f32) + row_ref[...])
            normed_ref[rows, :] = (hat * gain_ref[...] + shift_ref[...]).astype(bf16)

    out_ref[...] = (dot(normed_ref[...], w_ref[...], NN) + bias_ref[...]).astype(bf16)


def project(x, row, gain, shift, w, bias, first):
    T, D = x.shape
    wide = 512
    steps = (w.shape[1] - first) // wide
    skip = first // wide
    vec = whole(1, D)
    return call(
        project_kernel, (steps,),
        [whole(T, D), vec, vec, vec, pl.BlockSpec((D, wide), lambda c: (0, c + skip)), pl.BlockSpec((1, wide), lambda c: (0, c + skip))],
        [held(T, D), pl.BlockSpec((T, wide), lambda c: (0, c))],
        [shape((T, D), bf16), shape((T, steps * wide), bf16)],
        2 * T * D * wide * steps, 10e6,
    )(x, row, gain, shift, w, bias)


def own_forward_kernel(q_ref, k_ref, v_ref, o_ref, lse_ref):
    T = q_ref.shape[0]
    c = HEAD_DIM ** -0.5 * LOG2E
    row = lax.broadcasted_iota(jnp.int32, (BLOCK, BLOCK), 0)
    col = lax.broadcasted_iota(jnp.int32, (BLOCK, BLOCK), 1)
    for i in range(T // BLOCK):
        rows = slice(i * BLOCK, (i + 1) * BLOCK)
        q = q_ref[rows, :]
        last = jnp.where(col <= row, dot(q, k_ref[rows, :], NT), -1e30)
        top = jnp.max(last, axis=1, keepdims=True)
        if i:
            s = dot(q, k_ref[:i * BLOCK, :], NT)
            top = jnp.maximum(top, jnp.max(s, axis=1, keepdims=True))
        top = top * c
        p = jnp.exp2(last * c - top)
        total = jnp.sum(p, axis=1, keepdims=True)
        o = dot(p.astype(bf16), v_ref[rows, :], NN)
        if i:
            p = jnp.exp2(s * c - top)
            total += jnp.sum(p, axis=1, keepdims=True)
            o += dot(p.astype(bf16), v_ref[:i * BLOCK, :], NN)
        o_ref[rows, :] = o / total
        lse_ref[rows, :] = jnp.broadcast_to(top + jnp.log2(total), (BLOCK, HEAD_DIM))


def early_forward_kernel(pos_ref, q_ref, k_ref, v_ref, o1_ref, lse1_ref, att_ref, rest_ref, row_ref):
    T = q_ref.shape[0]
    c = HEAD_DIM ** -0.5 * LOG2E
    shut = jnp.where(pos_ref[0] > 0, 0.0, -1e30).astype(f32)
    for i in range(T // BLOCK):
        rows = slice(i * BLOCK, (i + 1) * BLOCK)
        s = dot(q_ref[rows, :], k_ref[...], NT)
        top = jnp.max(s, axis=1, keepdims=True) * c
        p = jnp.exp2(s * c - top)
        total = jnp.sum(p, axis=1, keepdims=True)
        o2 = dot(p.astype(bf16), v_ref[...], NN) / total
        lse2 = jnp.broadcast_to(top + jnp.log2(total) + shut, (BLOCK, HEAD_DIM))
        lse1 = lse1_ref[rows, :]
        high = jnp.maximum(lse1, lse2)
        w1, w2 = jnp.exp2(lse1 - high), jnp.exp2(lse2 - high)
        both = w1 + w2
        o = (o1_ref[rows, :] * w1 + o2 * w2) / both
        low = o.astype(bf16)
        att_ref[rows, :] = low
        rest_ref[rows, :] = (o - low.astype(f32)).astype(bf16)
        row_ref[0, :, rows] = jnp.transpose(high + jnp.log2(both))[:8, :]


def head_spec(T, skip=0):
    return pl.BlockSpec((T, HEAD_DIM), lambda h: (0, h + skip))


def row_spec(T):
    return pl.BlockSpec((1, 8, T), lambda h: (h, 0, 0))


def own_forward(joined, D):
    T = joined.shape[0]
    H = D // HEAD_DIM
    return call(
        own_forward_kernel, (H,), [head_spec(T), head_spec(T, H), head_spec(T, 2 * H)], [head_spec(T)] * 2,
        [shape((T, D), f32), shape((T, D), f32)], 12e9, 10e6,
    )(joined, joined, joined)


def early_forward(pos, joined, joined_e, o1, lse1):
    T, D = o1.shape
    H = D // HEAD_DIM
    return call(
        early_forward_kernel, (H,),
        [SMEM, head_spec(T), head_spec(T), head_spec(T, H), head_spec(T), head_spec(T)], [head_spec(T), head_spec(T), row_spec(T)],
        [shape((T, D), bf16), shape((T, D), bf16), shape((H, 8, T), f32)], 20e9, 12e6,
    )(pos, joined, joined_e, joined_e, o1, lse1)


def backward_kernel(causal, pos_ref, q_ref, k_ref, v_ref, do_ref, delta_ref, lse_ref, *refs):
    T = q_ref.shape[0]
    scale = HEAD_DIM ** -0.5
    c = scale * LOG2E
    do = do_ref[...]
    delta = delta_ref[pl.ds(pl.program_id(0), 1), :]
    lse = lse_ref[0, :1, :]
    if causal:
        dq_in, out_ref, dq_acc = refs
        key = lax.broadcasted_iota(jnp.int32, (BLOCK, BLOCK), 0)
        qry = lax.broadcasted_iota(jnp.int32, (BLOCK, BLOCK), 1)
        base = 1
    else:
        dq_out, out_ref, dq_acc = refs
        lse = lse + jnp.where(pos_ref[0] > 0, 0.0, 1e30).astype(f32)
        base = 0
    n = T // BLOCK
    for j in range(n):
        rows = slice(j * BLOCK, (j + 1) * BLOCK)
        a = j * BLOCK if causal else 0
        k = k_ref[rows, :]
        q = q_ref[a:, :]
        s = dot(k, q, NT)
        p = jnp.exp2(s * c - lse[:, a:])
        if causal:
            first = jnp.where(key <= qry, p[:, :BLOCK], 0.0)
            p = first if j == n - 1 else jnp.concatenate([first, p[:, BLOCK:]], axis=1)
        dp = dot(v_ref[rows, :], do[a:, :], NT)
        ds = (p * (dp - delta[:, a:])).astype(bf16)
        out_ref[base + 1, rows, :] = dot(p.astype(bf16), do[a:, :], NN).astype(bf16)
        out_ref[base, rows, :] = (dot(ds, q, NN) * scale).astype(bf16)
        part = jnp.transpose(dot(k, ds, TN))
        if j == 0:
            dq_acc[...] = part
        else:
            dq_acc[a:, :] += part
    dq = dq_acc[...] * scale
    if causal:
        out_ref[0] = (dq + dq_in[...]).astype(bf16)
    else:
        dq_out[...] = dq


def parts_spec(n, T):
    return pl.BlockSpec((n, T, HEAD_DIM), lambda h: (0, 0, h))


def early_backward(pos, joined, joined_e, do, delta, lse):
    T, D = do.shape
    H = D // HEAD_DIM
    return call(
        functools.partial(backward_kernel, False), (H,),
        [SMEM, head_spec(T), head_spec(T), head_spec(T, H), head_spec(T), whole(H, T), row_spec(T)],
        [head_spec(T), parts_spec(2, T)],
        [shape((T, D), f32), shape((2, T, D), bf16)], 26e9, 14e6, [pltpu.VMEM((T, HEAD_DIM), f32)],
    )(pos, joined, joined_e, joined_e, do, delta, lse)


def own_backward(pos, joined, do, delta, lse, dq):
    T, D = do.shape
    H = D // HEAD_DIM
    return call(
        functools.partial(backward_kernel, True), (H,),
        [SMEM, head_spec(T), head_spec(T, H), head_spec(T, 2 * H), head_spec(T), whole(H, T), row_spec(T), head_spec(T)],
        parts_spec(3, T), shape((3, T, D), bf16), 22e9, 14e6, [pltpu.VMEM((T, HEAD_DIM), f32)],
    )(pos, joined, joined, joined, do, delta, lse, dq)


def ffn_kernel(x_ref, row_ref, att_ref, rest_ref, wo_ref, bo_ref, gain_ref, shift_ref, up_ref, bup_ref, down_ref, bdown_ref, g_ref,
               out_ref, dmid_ref, datt_ref, branch_ref, n2_ref, act_ref, gup_ref, delta_ref, sums_ref, bup_sum_ref, mid, total, dn2):
    step = pl.program_id(0)
    T = x_ref.shape[0]
    blocks = [slice(i * BLOCK, (i + 1) * BLOCK) for i in range(T // BLOCK)]

    @pl.when(step == 0)
    def _():
        for rows in blocks:
            m = x_ref[rows, :].astype(f32) + row_ref[...] + (dot(att_ref[rows, :], wo_ref[...], NN) + bo_ref[...])
            mid[rows, :] = m
            hat, _ = ln_parts(m)
            n2_ref[rows, :] = (hat * gain_ref[...] + shift_ref[...]).astype(bf16)

    sums = None
    for rows in blocks:
        u = dot(n2_ref[rows, :], up_ref[...], NN) + bup_ref[...]
        cdf = 0.5 * (1.0 + lax.erf(u * 0.7071067811865476))
        pdf = jnp.exp(-0.5 * u * u) * 0.3989422804014327
        act = (u * cdf).astype(bf16)
        act_ref[rows, :] = act
        d_act = dot(g_ref[rows, :], down_ref[...], NT)
        gup = (d_act * (cdf + u * pdf)).astype(bf16)
        gup_ref[rows, :] = gup
        part = col_sum(gup)
        sums = part if sums is None else sums + part
        add = dot(act, down_ref[...], NN)
        back = dot(gup, up_ref[...], NT)

        @pl.when(step == 0)
        def _():
            total[rows, :] = add
            dn2[rows, :] = back

        @pl.when(step > 0)
        def _():
            total[rows, :] += add
            dn2[rows, :] += back

    bup_sum_ref[...] = sums

    @pl.when(step == pl.num_programs(0) - 1)
    def _():
        parts = None
        H, D = delta_ref.shape[0], x_ref.shape[1]
        head = lax.broadcasted_iota(jnp.int32, (H, D), 0)
        heads = (lax.broadcasted_iota(jnp.int32, (H, D), 1) // HEAD_DIM == head).astype(bf16)
        for rows in blocks:
            m = mid[rows, :]
            out_ref[rows, :] = (m + (total[rows, :] + bdown_ref[...])).astype(bf16)
            hat, rstd = ln_parts(m)
            grad = dn2[rows, :]
            g = g_ref[rows, :].astype(f32)
            d = g + ln_back(grad, hat, rstd, gain_ref[...])
            dmid_ref[rows, :] = d
            low = d.astype(bf16)
            branch_ref[rows, :] = low
            datt = dot(low, wo_ref[...], NT).astype(bf16)
            datt_ref[rows, :] = datt
            prod = datt.astype(f32) * (att_ref[rows, :].astype(f32) + rest_ref[rows, :].astype(f32))
            high = prod.astype(bf16)
            delta_ref[:, rows] = dot(heads, high, NT) + dot(heads, (prod - high.astype(f32)).astype(bf16), NT)
            new = [col_sum(low), col_sum(grad * hat), col_sum(grad), col_sum(g)]
            parts = new if parts is None else [a + b for a, b in zip(parts, new)]
        sums_ref[...] = jnp.zeros(sums_ref.shape, f32)
        for i, p in enumerate(parts):
            sums_ref[i:i + 1, :] = p


def ffn(x, row, att, rest, wo, bo, gain, shift, w_up, b_up, w_down, b_down, g):
    T, D = x.shape
    F = w_up.shape[1]
    wide = 512
    vec = whole(1, D)
    cols = pl.BlockSpec((T, wide), lambda f: (0, f))
    bias = pl.BlockSpec((1, wide), lambda f: (0, f))
    return call(
        ffn_kernel, (F // wide,),
        [whole(T, D), vec, whole(T, D), whole(T, D), whole(D, D), vec, vec, vec, pl.BlockSpec((D, wide), lambda f: (0, f)), bias,
         pl.BlockSpec((wide, D), lambda f: (f, 0)), vec, whole(T, D)],
        [held(T, D)] * 5 + [cols, cols, held(D // HEAD_DIM, T), held(8, D), bias],
        [shape((T, D), bf16), shape((T, D), f32), shape((T, D), bf16), shape((T, D), bf16), shape((T, D), bf16),
         shape((T, F), bf16), shape((T, F), bf16), shape((D // HEAD_DIM, T), f32), shape((8, D), f32), shape((1, F), f32)],
        2 * T * D * (2 * D + 4 * F) * 1.5, 30e6, [pltpu.VMEM((T, D), f32)] * 3,
    )(x, row, att, rest, wo, bo, gain, shift, w_up, b_up, w_down, b_down, g)


def grads_kernel(rows, terms, lefts, has_small, core_ref, place_ref, *refs):
    left, refs = refs[:lefts], refs[lefts:]
    mine_ref, theirs_ref, acc = refs[-3:]
    core = core_ref[0]
    first = pl.program_id(0) * (acc.shape[0] // 2)
    lane = mine_ref.shape[2]
    at = base = 0
    for group in terms:
        total = None
        for a in group:
            b = refs[at][0] if len(refs[at].shape) == 3 else refs[at][...]
            at += 1
            add = dot(left[a][...], b, TN)
            total = add if total is None else total + add
        acc[...] = total.reshape(acc.shape)
        for h in range(acc.shape[2] // lane):
            cols = slice(h * lane, (h + 1) * lane)
            for i in range(acc.shape[0] // 2):
                own = place_ref[core, first + i]
                other = place_ref[1 - core, first + i]
                mine_ref[own, base:base + rows, :] = acc[2 * i + core, :, cols].astype(bf16)
                theirs_ref[other, base:base + rows, :] = acc[2 * i + 1 - core, :, cols].astype(bf16)
            base += rows
    if has_small:
        small = refs[at]

        @pl.when(pl.program_id(0) == 0)
        def _():
            for i in range(mine_ref.shape[0]):
                mine_ref[place_ref[core, i], base:, :] = small[2 * i + core]
                theirs_ref[place_ref[1 - core, i], base:, :] = small[2 * i + 1 - core]


def grads(core, place, lefts, terms, devices, total_rows, row_block, block_rows, into=None, small=None):
    T, R = lefts[0].shape
    rows = R // devices
    steps = 4
    lane = 1024
    flat = [term for group in terms for term in group]
    ins = [core, place] + list(lefts)
    specs = [SMEM, SMEM] + [pl.BlockSpec((T, R // steps), lambda s: (0, s))] * len(lefts)
    for _, array, part in flat:
        ins.append(array)
        if array.ndim == 3:
            specs.append(pl.BlockSpec((1,) + array.shape[1:], lambda s, p=part: (p, 0, 0), pipeline_mode=pl.Buffered(1)))
        else:
            specs.append(whole(*array.shape))
    if small is not None:
        ins.append(small)
        specs.append(whole(*small.shape))
    aliases = {}
    if into is not None:
        aliases = {len(ins): 0, len(ins) + 1: 1}
        ins += list(into)
        specs += [pl.BlockSpec(memory_space=pl.ANY)] * 2
    kernel = functools.partial(grads_kernel, rows, [[a for a, _, _ in group] for group in terms], len(lefts), small is not None)
    width = flat[0][1].shape[-1]
    block = pl.BlockSpec((devices // 2, block_rows, lane), lambda s: (0, row_block, 0))
    out = shape((devices // 2, total_rows, lane), bf16)
    return call(
        kernel, (steps,), specs, [block, block], [out, out], 3 * T * R * width * len(flat), 20e6,
        [pltpu.VMEM((devices // steps, rows, width), f32)], aliases=aliases,
    )(*ins)


def plain_grads(lefts, terms, devices):
    out = []
    for group in terms:
        total = sum(dot(lefts[a], b if b.ndim == 2 else b[p], TN) for a, b, p in group).astype(bf16)
        lane = 1024
        split = total.reshape(devices, -1, total.shape[1] // lane, lane).transpose(0, 2, 1, 3)
        out.append(split.reshape(devices, -1, lane))
    return jnp.concatenate(out, axis=1)


def back_kernel(own, *refs):
    if own:
        x_ref, row_ref, gain_ref, dj_ref, w_ref, dmid_ref, out_ref, sums_ref, col_ref, dn = refs
    else:
        x_ref, row_ref, gain_ref, dj_ref, w_ref, out_ref, sums_ref, col_ref, dn = refs
    step = pl.program_id(0)
    dj = dj_ref[0]
    col_ref[...] = col_sum(dj)
    part = dot(dj, w_ref[...], NT)

    @pl.when(step == 0)
    def _():
        dn[...] = part

    @pl.when(step > 0)
    def _():
        dn[...] += part

    @pl.when(step == pl.num_programs(0) - 1)
    def _():
        parts = None
        for i in range(x_ref.shape[0] // BLOCK):
            rows = slice(i * BLOCK, (i + 1) * BLOCK)
            hat, rstd = ln_parts(x_ref[rows, :].astype(f32) + row_ref[...])
            grad = dn[rows, :]
            d = ln_back(grad, hat, rstd, gain_ref[...])
            if own:
                d = d + dmid_ref[rows, :]
            out_ref[rows, :] = d.astype(out_ref.dtype)
            new = [col_sum(d), col_sum(grad * hat), col_sum(grad)]
            parts = new if parts is None else [a + b for a, b in zip(parts, new)]
        sums_ref[...] = jnp.zeros(sums_ref.shape, f32)
        for i, p in enumerate(parts):
            sums_ref[i:i + 1, :] = p


def back(x, row, gain, dj, w, first, dmid=None):
    T, D = x.shape
    n = dj.shape[0]
    wide = 512
    per, skip = D // wide, first // wide
    vec = whole(1, D)
    own = dmid is not None
    ins = [x, row, gain, dj, w] + ([dmid] if own else [])
    specs = [whole(T, D), vec, vec, pl.BlockSpec((1, T, wide), lambda c: (c // per, 0, c % per)),
             pl.BlockSpec((D, wide), lambda c: (0, c + skip))] + ([whole(T, D)] if own else [])
    return call(
        functools.partial(back_kernel, own), (n * per,), specs,
        [held(T, D), held(8, D), pl.BlockSpec((1, wide), lambda c: (0, c))],
        [shape((T, D), f32 if own else bf16), shape((8, D), f32), shape((1, n * D), f32)],
        2 * T * D * n * D * 1.5, 16e6, [pltpu.VMEM((T, D), f32)],
    )(*ins)


class Scatter:
    def __init__(self, mesh):
        self.seq, self.dp = mesh.shape["seq"], mesh.shape["dp"]
        bits = []
        step = 2
        while step < self.dp:
            bits.append(step)
            step *= 2
        self.orders = [[0] + bits, bits + [0]]
        self.stages = len(bits) + 1
        self.count = 1 << self.stages

    def block(self, core, place):
        s, d = 0, core
        for k, bit in enumerate(self.orders[core]):
            on = (place >> (self.stages - 1 - k)) & 1
            if bit == 0:
                s = on
            else:
                d += bit * on
        return s * self.dp + d

    def places(self):
        table = [[0] * self.count for _ in range(2)]
        for c in range(2):
            for p in range(self.count):
                table[c][self.block(c, p) // 2] = p
        return jnp.array(table, jnp.int32)

    def mine_theirs(self, grad):
        core = lax.axis_index("dp") % 2
        pick = [grad[jnp.array([self.block(c, p) for p in range(self.count)])] for c in range(2)]
        return jnp.where(core == 0, pick[0], pick[1]), jnp.where(core == 0, pick[1], pick[0])

    def start(self, mine, theirs):
        return mine, lax.ppermute(theirs, "dp", [(i, i ^ 1) for i in range(self.dp)])

    def step(self, k, mine, got):
        d = lax.axis_index("dp")
        s = lax.axis_index("seq")
        core = d % 2
        pairs = []
        for a in range(self.seq):
            for b in range(self.dp):
                bit = self.orders[b % 2][k]
                to = ((1 - a) * self.dp + b) if bit == 0 else (a * self.dp + (b ^ bit))
                pairs.append((a * self.dp + b, to))
        own = [s if o[k] == 0 else (d // o[k]) % 2 for o in self.orders]
        own = jnp.where(core == 0, own[0], own[1])
        half = mine.shape[0] // 2

        def added(at):
            one = lax.dynamic_slice_in_dim(mine, at * half, half, 0).astype(f32)
            two = lax.dynamic_slice_in_dim(got, at * half, half, 0).astype(f32)
            return (one + two).astype(bf16)

        send, keep = added(1 - own), added(own)
        return keep, lax.ppermute(send, ("seq", "dp"), pairs)

    def finish(self, first, mine, got):
        for k in range(first, self.stages):
            mine, got = self.step(k, mine, got)
        return mine[0].astype(f32) + got[0].astype(f32)


def tie(state, *others):
    out = lax.optimization_barrier(tuple(state) + others)
    return out[:len(state)], out[len(state):]


def make_local(mesh):
    scatter = Scatter(mesh)
    devices = scatter.seq * scatter.dp

    def local(tokens, domain, domain_table, gain_one, shift_one, wqkv, bias_q, bias_v, w_out, b_out,
              gain_two, shift_two, w_up, b_up, w_down, b_down, cotangent):
        _, T, D = tokens.shape
        F = w_up.shape[1]
        share, ff = D // devices, F // devices
        kernels = share % 16 == 0
        packed = jnp.concatenate([
            gain_one, shift_one, b_out, gain_two, shift_two, b_down, b_up, bias_q, jnp.zeros((D,), bf16), bias_v,
            domain_table[domain[0]]]).astype(f32)[None, :]
        packed = lax.optimization_barrier(packed)
        gain_one, shift_one, b_out, gain_two, shift_two, b_down = (packed[:, i * D:(i + 1) * D] for i in range(6))
        b_up = packed[:, 6 * D:6 * D + F]
        bias = packed[:, 6 * D + F:9 * D + F]
        row = packed[:, 9 * D + F:]
        pos = lax.axis_index("seq").astype(jnp.int32)[None]
        core = (lax.axis_index("dp") % 2).astype(jnp.int32)[None]
        place = scatter.places()
        x, g = tokens[0], cotangent[0]
        early_x = lax.ppermute(x, "seq", [(0, 1)])

        normed, joined = project(x, row, gain_one, shift_one, wqkv, bias, 0)
        o1, lse1 = own_forward(joined, D)
        normed_e, joined_e = project(early_x, row, gain_one, shift_one, wqkv, bias, D)
        attended, rest, lse = early_forward(pos, joined, joined_e, o1, lse1)
        output, d_mid, d_att, branch, n2, active, g_upper, delta, sums_two, bup_sum = ffn(
            x, row, attended, rest, w_out, b_out, gain_two, shift_two, w_up, b_up, w_down, b_down, g)
        rows_a = ff + 2 * share + share
        if kernels:
            a = grads(core, place, [active], [[(0, g, 0)]], devices, rows_a, 0, ff)
            a = grads(core, place, [n2], [[(0, g_upper, 0)]], devices, rows_a, ff // (2 * share), 2 * share, into=a)
            a = grads(core, place, [attended], [[(0, branch, 0)]], devices, rows_a, (ff + 2 * share) // share, share, into=a)
        else:
            a = scatter.mine_theirs(jnp.concatenate([
                plain_grads([active], [[(0, g, 0)]], devices),
                plain_grads([n2], [[(0, g_upper, 0)]], devices),
                plain_grads([attended], [[(0, branch, 0)]], devices)], axis=1))
        a, (d_att,) = tie(a, d_att)
        a = scatter.start(*a)
        dq_e, dj_e = early_backward(pos, joined, joined_e, d_att, delta, lse)
        a, (dj_e,) = tie(a, dj_e)
        a = scatter.step(0, *a)
        dln_e, sums_e, col_e = back(early_x, row, gain_one, dj_e, wqkv, D)
        from_late = lax.ppermute(dln_e, "seq", [(1, 0)])
        dj = own_backward(pos, joined, d_att, delta, lse, dq_e)
        a, (dj,) = tie(a, dj)
        a = scatter.step(1, *a)
        base, sums_one, col = back(x, row, gain_one, dj, wqkv, 0, d_mid)
        a, (sums_one,) = tie(a, sums_one)
        a = scatter.step(2, *a)
        grad_tokens = (base + from_late.astype(f32)).astype(bf16)[None]

        sums_one = sums_one + sums_e
        domains = domain_table.shape[0]
        onehot = (jnp.arange(domains, dtype=jnp.int32) == domain[0]).astype(f32)
        small = jnp.concatenate([
            onehot[:, None] * sums_one[:1], sums_one[1:3], col[:, :D], col[:, 2 * D:] + col_e[:, D:], sums_two[:4]], axis=0)
        small = small.reshape(-1, devices, share).transpose(1, 0, 2).reshape(devices, -1)
        small = jnp.concatenate([small, bup_sum.reshape(devices, -1)], axis=1)
        small = jnp.pad(small, ((0, 0), (0, 16 * D - small.shape[1]))).reshape(devices, 16, D).astype(bf16)
        terms = [[(0, dj, 0)], [(0, dj, 1), (1, dj_e, 0)], [(0, dj, 2), (1, dj_e, 1)]]
        rows_b = 3 * share + 16
        if kernels:
            b = grads(core, place, [normed, normed_e], terms, devices, rows_b, 0, rows_b, small=small)
        else:
            b = scatter.mine_theirs(jnp.concatenate([plain_grads([normed, normed_e], terms, devices), small], axis=1))
        a, b = tie(a, *b)
        sum_a = scatter.finish(3, *a)
        sum_b = scatter.finish(0, *scatter.start(*b))

        join = lambda a, n: jnp.concatenate([a[i * share:(i + 1) * share] for i in range(n)], axis=1)
        flat = sum_b[3 * share:].reshape(-1)
        piece = lambda i: flat[i * share:(i + 1) * share]
        m = domains
        return (
            output[None], grad_tokens, flat[:m * share].reshape(m, share), piece(m), piece(m + 1), join(sum_b, 3),
            piece(m + 2), piece(m + 3), sum_a[ff + 2 * share:], piece(m + 4), piece(m + 5), piece(m + 6),
            join(sum_a[ff:], 2), flat[(m + 8) * share:(m + 8) * share + ff], sum_a[:ff], piece(m + 7))

    return local


def solution(mesh):
    both = ("seq", "dp")
    lead, rows = P("dp", "seq", None), P(both, None)
    return jax.shard_map(
        make_local(mesh),
        mesh=mesh,
        in_specs=(lead, P("dp")) + (P(),) * 14 + (lead,),
        out_specs=(lead, lead, P(None, both), P(both), P(both), rows, P(both), P(both), rows, P(both), P(both), P(both),
                   rows, P(both), rows, P(both)),
        check_vma=False,
    )
```

```python
import functools

import jax
import jax.numpy as jnp
from jax import lax
from jax.experimental import pallas as pl
from jax.experimental.pallas import tpu as pltpu
from jax.sharding import PartitionSpec as P

HEAD_DIM = 128
EPSILON = 1e-05
LOG2E = 1.4426950408889634
BLOCK = 256
MIB = 20
COST = 0.05
MIB_FFN = 34
f32, bf16 = jnp.float32, jnp.bfloat16
NN = ((1,), (0,))
NT = ((1,), (1,))
TN = ((0,), (0,))
ROW, GAIN_ONE, SHIFT_ONE, BIAS, B_OUT, GAIN_TWO, SHIFT_TWO, B_DOWN, B_UP = 0, 1, 2, 3, 6, 7, 8, 9, 10
SMEM = pl.BlockSpec(memory_space=pltpu.SMEM)


def dot(a, b, dims):
    return lax.dot_general(a, b, (dims, ((), ())), preferred_element_type=f32)


def call(kernel, grid, in_specs, out_specs, out_shape, flops, moved, scratch=(), mib=MIB, aliases=None):
    return pl.pallas_call(
        kernel,
        grid=grid,
        in_specs=in_specs,
        out_specs=out_specs,
        out_shape=out_shape,
        scratch_shapes=list(scratch),
        input_output_aliases=aliases or {},
        cost_estimate=pl.CostEstimate(flops=int(flops * COST), bytes_accessed=int(moved * COST), transcendentals=0),
        compiler_params=pltpu.CompilerParams(vmem_limit_bytes=mib * 2**20),
    )


def shape(dims, kind):
    return jax.ShapeDtypeStruct(dims, kind)


def near(dims, kind):
    return pltpu.VMEM(dims, kind)


def far(dims, kind):
    return pltpu.HBM(dims, kind)


def in_vmem(*arrays):
    return [pltpu.with_memory_space_constraint(a, pltpu.VMEM) for a in arrays]


def in_hbm(*arrays):
    return [pltpu.with_memory_space_constraint(a, pltpu.HBM) for a in arrays]


def whole(*dims):
    return pl.BlockSpec(dims, lambda *_: (0,) * len(dims), pipeline_mode=pl.Buffered(1))


def held(*dims):
    return pl.BlockSpec(dims, lambda *_: (0,) * len(dims))


def ln_parts(x):
    center = x - jnp.mean(x, axis=-1, keepdims=True)
    rstd = lax.rsqrt(jnp.mean(center * center, axis=-1, keepdims=True) + EPSILON)
    return center * rstd, rstd


def ln_back(grad, hat, rstd, gain):
    g = grad * gain
    return rstd * (g - jnp.mean(g, axis=-1, keepdims=True) - hat * jnp.mean(g * hat, axis=-1, keepdims=True))


def col_sum(a):
    return jnp.sum(a.astype(f32), axis=0, keepdims=True)


def project_kernel(first, x_ref, vec_ref, w_ref, normed_ref, out_ref):
    @pl.when(pl.program_id(0) == 0)
    def _():
        for i in range(x_ref.shape[0] // BLOCK):
            rows = slice(i * BLOCK, (i + 1) * BLOCK)
            hat, _ = ln_parts(x_ref[rows, :].astype(f32) + vec_ref[ROW:ROW + 1, :])
            normed_ref[rows, :] = (hat * vec_ref[GAIN_ONE:GAIN_ONE + 1, :] + vec_ref[SHIFT_ONE:SHIFT_ONE + 1, :]).astype(bf16)

    wide = w_ref.shape[1]
    at = first + pl.program_id(0) * wide
    lane = x_ref.shape[1]
    bias = vec_ref[pl.ds(BIAS + at // lane, 1), pl.ds(pl.multiple_of(at % lane, wide), wide)]
    out_ref[...] = (dot(normed_ref[...], w_ref[...], NN) + bias).astype(bf16)


def project(x, vectors, w, first):
    T, D = x.shape
    wide = 512
    steps = (w.shape[1] - first) // wide
    skip = first // wide
    return call(
        functools.partial(project_kernel, first), (steps,),
        [whole(T, D), whole(*vectors.shape), pl.BlockSpec((D, wide), lambda c: (0, c + skip))],
        [held(T, D), pl.BlockSpec((T, wide), lambda c: (0, c))],
        [far((T, D), bf16), near((T, steps * wide), bf16)],
        2 * T * D * wide * steps, 10e6,
    )(x, vectors, *in_hbm(w))


def own_forward_kernel(q_ref, k_ref, v_ref, o_ref, lse_ref):
    T = q_ref.shape[0]
    c = HEAD_DIM ** -0.5 * LOG2E
    row = lax.broadcasted_iota(jnp.int32, (BLOCK, BLOCK), 0)
    col = lax.broadcasted_iota(jnp.int32, (BLOCK, BLOCK), 1)
    for i in range(T // BLOCK):
        for h in range(q_ref.shape[1] // HEAD_DIM):
            rows, head = slice(i * BLOCK, (i + 1) * BLOCK), slice(h * HEAD_DIM, (h + 1) * HEAD_DIM)
            q = q_ref[rows, head]
            last = jnp.where(col <= row, dot(q, k_ref[rows, head], NT), -1e30)
            top = jnp.max(last, axis=1, keepdims=True)
            if i:
                s = dot(q, k_ref[:i * BLOCK, head], NT)
                top = jnp.maximum(top, jnp.max(s, axis=1, keepdims=True))
            top = top * c
            p = jnp.exp2(last * c - top)
            total = jnp.sum(p, axis=1, keepdims=True)
            o = dot(p.astype(bf16), v_ref[rows, head], NN)
            if i:
                p = jnp.exp2(s * c - top)
                total += jnp.sum(p, axis=1, keepdims=True)
                o += dot(p.astype(bf16), v_ref[:i * BLOCK, head], NN)
            o_ref[rows, head] = o / total
            lse_ref[rows, head] = jnp.broadcast_to(top + jnp.log2(total), (BLOCK, HEAD_DIM))


def early_forward_kernel(pos_ref, q_ref, k_ref, v_ref, o1_ref, lse1_ref, att_ref, rest_ref, row_ref):
    T = q_ref.shape[0]
    c = HEAD_DIM ** -0.5 * LOG2E
    shut = jnp.where(pos_ref[0] > 0, 0.0, -1e30).astype(f32)
    units = [(i, h) for i in range(T // BLOCK) for h in range(q_ref.shape[1] // HEAD_DIM)]

    def scores(i, h):
        head = slice(h * HEAD_DIM, (h + 1) * HEAD_DIM)
        return dot(q_ref[i * BLOCK:(i + 1) * BLOCK, head], k_ref[:, head], NT)

    ahead = scores(*units[0])
    for n, (i, h) in enumerate(units):
        rows, head = slice(i * BLOCK, (i + 1) * BLOCK), slice(h * HEAD_DIM, (h + 1) * HEAD_DIM)
        s = ahead
        if n + 1 < len(units):
            ahead = scores(*units[n + 1])
        top = jnp.max(s, axis=1, keepdims=True) * c
        p = jnp.exp2(s * c - top)
        total = jnp.sum(p, axis=1, keepdims=True)
        o2 = dot(p.astype(bf16), v_ref[:, head], NN) / total
        lse2 = jnp.broadcast_to(top + jnp.log2(total) + shut, (BLOCK, HEAD_DIM))
        lse1 = lse1_ref[rows, head]
        high = jnp.maximum(lse1, lse2)
        w1, w2 = jnp.exp2(lse1 - high), jnp.exp2(lse2 - high)
        both = w1 + w2
        o = (o1_ref[rows, head] * w1 + o2 * w2) / both
        low = o.astype(bf16)
        att_ref[rows, head] = low
        rest_ref[rows, head] = (o - low.astype(f32)).astype(bf16)
        row_ref[h, :, rows] = jnp.transpose(high + jnp.log2(both))[:8, :]


def head_spec(T, skip=0):
    return pl.BlockSpec((T, HEAD_DIM), lambda h: (0, h + skip))


def row_spec(T):
    return pl.BlockSpec((1, 8, T), lambda h: (h, 0, 0))


def heads_spec(T, many, skip=0):
    return pl.BlockSpec((T, many * HEAD_DIM), lambda h: (0, h + skip))


def own_forward(joined, D):
    T = joined.shape[0]
    many = 4
    H = D // HEAD_DIM // many
    spec = functools.partial(heads_spec, T, many)
    return call(
        own_forward_kernel, (H,), [spec(), spec(H), spec(2 * H)], [spec(), spec()],
        [near((T, D), f32), near((T, D), f32)], 12e9, 10e6,
    )(*in_vmem(joined, joined, joined))


def early_forward(pos, joined, joined_e, o1, lse1):
    T, D = o1.shape
    many = 4
    H = D // HEAD_DIM // many
    spec = functools.partial(heads_spec, T, many)
    return call(
        early_forward_kernel, (H,), [SMEM, spec(), spec(), spec(H), spec(), spec()],
        [spec(), spec(), pl.BlockSpec((many, 8, T), lambda h: (h, 0, 0))],
        [near((T, D), bf16), near((T, D), bf16), near((H * many, 8, T), f32)], 20e9, 12e6,
    )(pos, *in_vmem(joined, joined_e, joined_e, o1, lse1))


def backward_kernel(causal, pos_ref, q_ref, k_ref, v_ref, do_ref, delta_ref, lse_ref, *refs):
    T = q_ref.shape[0]
    scale = HEAD_DIM ** -0.5
    c = scale * LOG2E
    do = do_ref[...]
    delta = delta_ref[pl.ds(pl.program_id(0), 1), :]
    lse = lse_ref[0, :1, :]
    if causal:
        dq_in, out_ref, dq_acc = refs
        key = lax.broadcasted_iota(jnp.int32, (BLOCK, BLOCK), 0)
        qry = lax.broadcasted_iota(jnp.int32, (BLOCK, BLOCK), 1)
        base = 1
    else:
        dq_out, out_ref, dq_acc = refs
        lse = lse + jnp.where(pos_ref[0] > 0, 0.0, 1e30).astype(f32)
        base = 0
    n = T // BLOCK
    for j in range(n):
        rows = slice(j * BLOCK, (j + 1) * BLOCK)
        a = j * BLOCK if causal else 0
        k = k_ref[rows, :]
        q = q_ref[a:, :]
        s = dot(k, q, NT)
        p = jnp.exp2(s * c - lse[:, a:])
        if causal:
            first = jnp.where(key <= qry, p[:, :BLOCK], 0.0)
            p = first if j == n - 1 else jnp.concatenate([first, p[:, BLOCK:]], axis=1)
        dp = dot(v_ref[rows, :], do[a:, :], NT)
        ds = (p * (dp - delta[:, a:])).astype(bf16)
        out_ref[base + 1, rows, :] = dot(p.astype(bf16), do[a:, :], NN).astype(bf16)
        out_ref[base, rows, :] = (dot(ds, q, NN) * scale).astype(bf16)
        part = jnp.transpose(dot(k, ds, TN))
        if j == 0:
            dq_acc[...] = part
        else:
            dq_acc[a:, :] += part
    dq = dq_acc[...] * scale
    if causal:
        out_ref[0] = (dq + dq_in[...]).astype(bf16)
    else:
        dq_out[...] = dq


def parts_spec(n, T):
    return pl.BlockSpec((n, T, HEAD_DIM), lambda h: (0, 0, h))


def early_backward(pos, joined, joined_e, do, delta, lse):
    T, D = do.shape
    H = D // HEAD_DIM
    return call(
        functools.partial(backward_kernel, False), (H,),
        [SMEM, head_spec(T), head_spec(T), head_spec(T, H), head_spec(T), whole(H, T), row_spec(T)],
        [head_spec(T), parts_spec(2, T)],
        [far((T, D), f32), near((2, T, D), bf16)], 26e9, 14e6, [pltpu.VMEM((T, HEAD_DIM), f32)],
    )(pos, *in_hbm(joined, joined_e, joined_e, do), *in_vmem(delta, lse))


def own_backward(pos, joined, do, delta, lse, dq):
    T, D = do.shape
    H = D // HEAD_DIM
    return call(
        functools.partial(backward_kernel, True), (H,),
        [SMEM, head_spec(T), head_spec(T, H), head_spec(T, 2 * H), head_spec(T), whole(H, T), row_spec(T), head_spec(T)],
        parts_spec(3, T), near((3, T, D), bf16), 22e9, 14e6, [pltpu.VMEM((T, HEAD_DIM), f32)],
    )(pos, *in_hbm(joined, joined, joined, do), *in_vmem(delta, lse), *in_hbm(dq))


def ffn_kernel(x_ref, att_ref, rest_ref, vec_ref, g_ref, dact_ref, wo_in, up_in, down_in,
               out_ref, dmid_ref, datt_ref, branch_ref, n2_ref, act_ref, gup_ref, delta_ref, sums_ref, bup_sum_ref,
               wo_ref, up_ref, down_ref, arrived):
    D, F, H = x_ref.shape[1], up_ref.shape[1], delta_ref.shape[0]
    first = pl.program_id(0) == 0
    copies = [pltpu.make_async_copy(a, b, arrived.at[i])
              for i, (a, b) in enumerate([(wo_in, wo_ref), (up_in, up_ref), (down_in, down_ref)])]

    @pl.when(first)
    def _():
        for copy in copies:
            copy.start()
        copies[0].wait()
        sums_ref[...] = jnp.zeros(sums_ref.shape, f32)
        bup_sum_ref[...] = jnp.zeros(bup_sum_ref.shape, f32)

    vec = lambda i: vec_ref[i:i + 1, :]
    m = x_ref[...].astype(f32) + vec(ROW) + (dot(att_ref[...], wo_ref[...], NN) + vec(B_OUT))
    hat, rstd = ln_parts(m)
    n2_ref[...] = (hat * vec(GAIN_TWO) + vec(SHIFT_TWO)).astype(bf16)

    @pl.when(first)
    def _():
        copies[1].wait()
        copies[2].wait()

    wide = 512
    for f in range(0, F, wide):
        cols = slice(f, f + wide)
        u = dot(n2_ref[...], up_ref[:, cols], NN) + vec(B_UP + f // D)[:, f % D:f % D + wide]
        d_act = dact_ref[:, cols].astype(f32)
        cdf = 0.5 * (1.0 + lax.erf(u * 0.7071067811865476))
        pdf = jnp.exp(-0.5 * u * u) * 0.3989422804014327
        act_ref[:, cols] = (u * cdf).astype(bf16)
        gup = (d_act * (cdf + u * pdf)).astype(bf16)
        gup_ref[:, cols] = gup
        bup_sum_ref[:, cols] += col_sum(gup)
    grad = dot(gup_ref[...], up_ref[...], NT)
    g = g_ref[...].astype(f32)
    d = g + ln_back(grad, hat, rstd, vec(GAIN_TWO))
    dmid_ref[...] = d
    low = d.astype(bf16)
    branch_ref[...] = low
    out_ref[...] = (m + (dot(act_ref[...], down_ref[...], NN) + vec(B_DOWN))).astype(bf16)
    datt = dot(low, wo_ref[...], NT).astype(bf16)
    datt_ref[...] = datt
    prod = datt.astype(f32) * (att_ref[...].astype(f32) + rest_ref[...].astype(f32))
    high = prod.astype(bf16)
    head = lax.broadcasted_iota(jnp.int32, (H, D), 0)
    heads = (lax.broadcasted_iota(jnp.int32, (H, D), 1) // HEAD_DIM == head).astype(bf16)
    delta_ref[...] = dot(heads, high, NT) + dot(heads, (prod - high.astype(f32)).astype(bf16), NT)
    for i, p in enumerate([col_sum(low), col_sum(grad * hat), col_sum(grad), col_sum(g)]):
        sums_ref[i:i + 1, :] += p


def ffn(x, att, rest, vectors, g, dact, wo, w_up, w_down):
    T, D = x.shape
    F = w_up.shape[1]
    H = D // HEAD_DIM
    part = lambda w: pl.BlockSpec((BLOCK, w), lambda i: (i, 0))
    return call(
        ffn_kernel, (T // BLOCK,),
        [part(D), part(D), part(D), whole(*vectors.shape), part(D), part(F)] + [pl.BlockSpec(memory_space=pltpu.HBM)] * 3,
        [part(D)] * 5 + [part(F), part(F), pl.BlockSpec((H, BLOCK), lambda i: (0, i)), held(8, D), held(1, F)],
        [far((T, D), bf16), far((T, D), f32), far((T, D), bf16), near((T, D), bf16), near((T, D), bf16),
         near((T, F), bf16), near((T, F), bf16), near((H, T), f32), shape((8, D), f32), shape((1, F), f32)],
        2 * T * D * (2 * D + 4 * F) * 1.5, 30e6,
        [pltpu.VMEM((D, D), bf16), pltpu.VMEM((D, F), bf16), pltpu.VMEM((F, D), bf16), pltpu.SemaphoreType.DMA((3,))], mib=MIB_FFN,
    )(x, *in_vmem(att, rest), vectors, g, dact, wo, w_up, w_down)


def times_kernel(a_ref, b_ref, out_ref):
    out_ref[...] = dot(a_ref[...], b_ref[...], NT).astype(bf16)


def times(a, b):
    T, D = a.shape
    F = b.shape[0]
    wide = 512
    return call(
        times_kernel, (F // wide,), [whole(T, D), pl.BlockSpec((wide, D), lambda f: (f, 0))], pl.BlockSpec((T, wide), lambda f: (0, f)),
        far((T, F), bf16), 2 * T * D * F, 8e6,
    )(*in_hbm(a, b))


def grads_kernel(rows, terms, lefts, core_ref, place_ref, *refs):
    left, refs = refs[:lefts], refs[lefts:]
    mine_ref, theirs_ref, acc = refs[-3:]
    core = core_ref[0]
    first = pl.program_id(0) * (acc.shape[0] // 2)
    lane = mine_ref.shape[2]
    at = base = 0
    for group in terms:
        total = None
        for a in group:
            b = refs[at][0] if len(refs[at].shape) == 3 else refs[at][...]
            at += 1
            add = dot(left[a][...], b, TN)
            total = add if total is None else total + add
        acc[...] = total.reshape(acc.shape)
        for h in range(acc.shape[2] // lane):
            cols = slice(h * lane, (h + 1) * lane)
            for i in range(acc.shape[0] // 2):
                own = place_ref[core, first + i]
                other = place_ref[1 - core, first + i]
                mine_ref[own, base:base + rows, :] = acc[2 * i + core, :, cols].astype(bf16)
                theirs_ref[other, base:base + rows, :] = acc[2 * i + 1 - core, :, cols].astype(bf16)
            base += rows


def grads(core, place, lefts, terms, devices, total_rows, row_block, block_rows, into=None):
    T, R = lefts[0].shape
    rows = R // devices
    steps = 4
    lane = 1024
    flat = [term for group in terms for term in group]
    ins = [core, place] + list(lefts)
    specs = [SMEM, SMEM] + [pl.BlockSpec((T, R // steps), lambda s: (0, s))] * len(lefts)
    for _, array, part in flat:
        ins.append(array)
        if array.ndim == 3:
            specs.append(pl.BlockSpec((1,) + array.shape[1:], lambda s, p=part: (p, 0, 0), pipeline_mode=pl.Buffered(1)))
        else:
            specs.append(whole(*array.shape))
    aliases = {}
    if into is not None:
        aliases = {len(ins): 0, len(ins) + 1: 1}
        ins += list(into)
        specs += [pl.BlockSpec(memory_space=pl.ANY)] * 2
    kernel = functools.partial(grads_kernel, rows, [[a for a, _, _ in group] for group in terms], len(lefts))
    width = flat[0][1].shape[-1]
    block = pl.BlockSpec((devices // 2, block_rows, lane), lambda s: (0, row_block, 0))
    out = shape((devices // 2, total_rows, lane), bf16)
    return call(
        kernel, (steps,), specs, [block, block], [out, out], 3 * T * R * width * len(flat), 20e6,
        [pltpu.VMEM((devices // steps, rows, width), f32)], aliases=aliases,
    )(*ins)


def plain_grads(lefts, terms, devices):
    out = []
    for group in terms:
        total = sum(dot(lefts[a], b if b.ndim == 2 else b[p], TN) for a, b, p in group).astype(bf16)
        lane = 1024
        split = total.reshape(devices, -1, total.shape[1] // lane, lane).transpose(0, 2, 1, 3)
        out.append(split.reshape(devices, -1, lane))
    return jnp.concatenate(out, axis=1)


def back_kernel(own, *refs):
    if own:
        x_ref, vec_ref, dj_ref, w_ref, dmid_ref, out_ref, sums_ref, col_ref, dn = refs
    else:
        x_ref, vec_ref, dj_ref, w_ref, out_ref, sums_ref, col_ref, dn = refs
    step = pl.program_id(0)
    dj = dj_ref[0]
    col_ref[...] = col_sum(dj)
    part = dot(dj, w_ref[...], NT)

    @pl.when(step == 0)
    def _():
        dn[...] = part

    @pl.when(step > 0)
    def _():
        dn[...] += part

    @pl.when(step == pl.num_programs(0) - 1)
    def _():
        parts = None
        for i in range(x_ref.shape[0] // BLOCK):
            rows = slice(i * BLOCK, (i + 1) * BLOCK)
            hat, rstd = ln_parts(x_ref[rows, :].astype(f32) + vec_ref[ROW:ROW + 1, :])
            grad = dn[rows, :]
            d = ln_back(grad, hat, rstd, vec_ref[GAIN_ONE:GAIN_ONE + 1, :])
            if own:
                d = d + dmid_ref[rows, :]
            out_ref[rows, :] = d.astype(out_ref.dtype)
            new = [col_sum(d), col_sum(grad * hat), col_sum(grad)]
            parts = new if parts is None else [a + b for a, b in zip(parts, new)]
        sums_ref[...] = jnp.zeros(sums_ref.shape, f32)
        for i, p in enumerate(parts):
            sums_ref[i:i + 1, :] = p


def back(x, vectors, dj, w, first, dmid=None):
    T, D = x.shape
    n = dj.shape[0]
    wide = 512
    per, skip = D // wide, first // wide
    own = dmid is not None
    ins = [*(in_hbm(x) if own else [x]), vectors, *in_vmem(dj), *in_hbm(w)] + (in_hbm(dmid) if own else [])
    specs = [whole(T, D), whole(*vectors.shape), pl.BlockSpec((1, T, wide), lambda c: (c // per, 0, c % per)),
             pl.BlockSpec((D, wide), lambda c: (0, c + skip))] + ([whole(T, D)] if own else [])
    return call(
        functools.partial(back_kernel, own), (n * per,), specs,
        [held(T, D), held(8, D), pl.BlockSpec((1, wide), lambda c: (0, c))],
        [far((T, D), f32 if own else bf16), shape((8, D), f32), shape((1, n * D), f32)],
        2 * T * D * n * D * 1.5, 16e6, [pltpu.VMEM((T, D), f32)], mib=24,
    )(*ins)


class Scatter:
    def __init__(self, mesh, x_first):
        self.seq, self.dp = mesh.shape["seq"], mesh.shape["dp"]
        bits = []
        step = 2
        while step < self.dp:
            bits.append(step)
            step *= 2
        if x_first:
            self.orders = [[0] + bits, bits + [0]]
        else:
            self.orders = [[bits[0], 0] + bits[1:], [bits[1], bits[0], 0] + bits[2:]]
        self.stages = len(bits) + 1
        self.count = 1 << self.stages

    def block(self, core, place):
        s, d = 0, core
        for k, bit in enumerate(self.orders[core]):
            on = (place >> (self.stages - 1 - k)) & 1
            if bit == 0:
                s = on
            else:
                d += bit * on
        return s * self.dp + d

    def places(self):
        table = [[0] * self.count for _ in range(2)]
        for c in range(2):
            for p in range(self.count):
                table[c][self.block(c, p) // 2] = p
        return jnp.array(table, jnp.int32)

    def mine_theirs(self, grad):
        core = lax.axis_index("dp") % 2
        pick = [grad[jnp.array([self.block(c, p) for p in range(self.count)])] for c in range(2)]
        return jnp.where(core == 0, pick[0], pick[1]), jnp.where(core == 0, pick[1], pick[0])

    def begin(self, mine, theirs):
        got = lax.ppermute(theirs, "dp", [(i, i ^ 1) for i in range(self.dp)])
        return [mine, got], [0, 0], self.count

    def pairs(self, k):
        pairs = []
        for a in range(self.seq):
            for b in range(self.dp):
                bit = self.orders[b % 2][k]
                to = ((1 - a) * self.dp + b) if bit == 0 else (a * self.dp + (b ^ bit))
                pairs.append((a * self.dp + b, to))
        return pairs

    def total(self, state, at, size):
        arrays, bases, _ = state
        return sum(lax.dynamic_slice_in_dim(a, base + at, size, 0).astype(f32) for a, base in zip(arrays, bases))

    def step(self, k, state):
        d = lax.axis_index("dp")
        core = d % 2
        own = [lax.axis_index("seq") if o[k] == 0 else (d // o[k]) % 2 for o in self.orders]
        own = jnp.where(core == 0, own[0], own[1])
        arrays, bases, size = state
        half = size // 2
        send = self.total(state, (1 - own) * half, half).astype(bf16)
        got = lax.ppermute(send, ("seq", "dp"), self.pairs(k))
        return (arrays + [got], [base + own * half for base in bases] + [0], half), send

    def finish(self, first, state):
        for k in range(first, self.stages):
            state, _ = self.step(k, state)
        return self.total(state, 0, 1)[0]


def after(value, *before):
    return lax.optimization_barrier((value,) + before)[0]


def after_state(state, *before):
    arrays, bases, size = state
    out = lax.optimization_barrier(tuple(arrays) + before)
    return list(out[:len(arrays)]), bases, size


def make_local(mesh):
    scatter, scatter_b = Scatter(mesh, False), Scatter(mesh, True)
    devices = scatter.seq * scatter.dp

    def local(tokens, domain, domain_table, gain_one, shift_one, wqkv, bias_q, bias_v, w_out, b_out,
              gain_two, shift_two, w_up, b_up, w_down, b_down, cotangent):
        _, T, D = tokens.shape
        F = w_up.shape[1]
        share, ff = D // devices, F // devices
        kernels = share % 16 == 0
        line = [domain_table[domain[0]], gain_one, shift_one, bias_q, None, bias_v, b_out, gain_two, shift_two, b_down]
        line += [b_up[i:i + D] for i in range(0, F, D)]
        at = lax.broadcasted_iota(jnp.int32, (16, D), 0)
        vectors = jnp.zeros((16, D), f32)
        for i, v in enumerate(line):
            if v is not None:
                vectors = jnp.where(at == i, v.astype(f32)[None, :], vectors)
        pos = lax.axis_index("seq").astype(jnp.int32)[None]
        core = (lax.axis_index("dp") % 2).astype(jnp.int32)[None]
        place, place_b = scatter.places(), scatter_b.places()
        x, g = tokens[0], cotangent[0]
        early_x = lax.ppermute(x, "seq", [(0, 1)])

        normed, joined = project(x, vectors, wqkv, 0)
        o1, lse1 = own_forward(joined, D)
        d_act = times(g, w_down)
        early_x, o1, d_act = lax.optimization_barrier((early_x, o1, d_act))
        normed_e, joined_e = project(early_x, vectors, wqkv, D)
        attended, rest, lse = early_forward(pos, joined, joined_e, o1, lse1)
        output, d_mid, d_att, branch, n2, active, g_upper, delta, sums_two, bup_sum = ffn(
            x, attended, rest, vectors, g, d_act, w_out, w_up, w_down)
        rows_a = ff + 2 * share + share
        if kernels:
            a = grads(core, place, [active], [[(0, g, 0)]], devices, rows_a, 0, ff)
            a = grads(core, place, [n2], [[(0, g_upper, 0)]], devices, rows_a, ff // (2 * share), 2 * share, into=a)
            a = grads(core, place, [attended], [[(0, branch, 0)]], devices, rows_a, (ff + 2 * share) // share, share, into=a)
        else:
            a = scatter.mine_theirs(jnp.concatenate([
                plain_grads([active], [[(0, g, 0)]], devices),
                plain_grads([n2], [[(0, g_upper, 0)]], devices),
                plain_grads([attended], [[(0, branch, 0)]], devices)], axis=1))
        a = scatter.begin(*a)
        dq_e, dj_e = early_backward(pos, joined, joined_e, after(d_att, a[0][0]), delta, lse)
        a, sent = scatter.step(0, after_state(a, dj_e))
        dln_e, sums_e, col_e = back(early_x, vectors, after(dj_e, sent), wqkv, D)
        from_late = lax.ppermute(dln_e, "seq", [(1, 0)])
        dj = own_backward(pos, joined, d_att, delta, lse, after(dq_e, sums_e))
        a, sent = scatter.step(1, after_state(a, dj))
        terms = [[(0, dj, 0)], [(0, dj, 1), (1, dj_e, 0)], [(0, dj, 2), (1, dj_e, 1)]]
        if kernels:
            b = grads(core, place_b, in_hbm(after(normed, sent), normed_e), terms, devices, 3 * share, 0, 3 * share)
        else:
            b = scatter_b.mine_theirs(plain_grads([normed, normed_e], terms, devices))
        b = [after(b[0], from_late), after(b[1], from_late)]
        b = scatter_b.begin(*b)
        b, sent = scatter_b.step(0, b)
        base, sums_one, col = back(x, vectors, after(dj, sent), wqkv, 0, d_mid)
        a, sent = scatter.step(2, after_state(a, base))

        sums_one = sums_one + sums_e
        domains = domain_table.shape[0]
        onehot = (jnp.arange(domains, dtype=jnp.int32) == domain[0]).astype(f32)
        small = jnp.concatenate([
            onehot[:, None] * sums_one[:1], sums_one[1:3], col[:, :D], col[:, 2 * D:] + col_e[:, D:], sums_two[:4]], axis=0)
        small = small.reshape(-1, devices, share).transpose(1, 0, 2).reshape(devices, -1)
        small = jnp.concatenate([small, bup_sum.reshape(devices, -1)], axis=1)
        flat = jnp.sum(lax.all_to_all(after(small, sent), ("seq", "dp"), 0, 0, tiled=True), axis=0)
        b, sent = scatter_b.step(1, after_state(b, flat))
        grad_tokens = (after(base, sent) + from_late.astype(f32)).astype(bf16)[None]
        a, sent = scatter.step(3, after_state(a, grad_tokens))
        b, sent = scatter_b.step(2, after_state(b, sent))
        b, sent = scatter_b.step(3, after_state(b, sent))
        sum_a = scatter.finish(4, after_state(a, sent))
        sum_b = scatter_b.finish(4, b)

        join = lambda a, n: jnp.concatenate([a[i * share:(i + 1) * share] for i in range(n)], axis=1)
        piece = lambda i: flat[i * share:(i + 1) * share]
        m = domains
        return (
            output[None], grad_tokens, flat[:m * share].reshape(m, share), piece(m), piece(m + 1), join(sum_b, 3),
            piece(m + 2), piece(m + 3), sum_a[ff + 2 * share:], piece(m + 4), piece(m + 5), piece(m + 6),
            join(sum_a[ff:], 2), flat[(m + 8) * share:(m + 8) * share + ff], sum_a[:ff], piece(m + 7))

    return local


def solution(mesh):
    both = ("seq", "dp")
    lead, rows = P("dp", "seq", None), P(both, None)
    return jax.shard_map(
        make_local(mesh),
        mesh=mesh,
        in_specs=(lead, P("dp")) + (P(),) * 14 + (lead,),
        out_specs=(lead, lead, P(None, both), P(both), P(both), rows, P(both), P(both), rows, P(both), P(both), P(both),
                   rows, P(both), rows, P(both)),
        check_vma=False,
    )
```

```python
import functools

import jax
import jax.numpy as jnp
from jax import lax
from jax.experimental import pallas as pl
from jax.experimental.pallas import tpu as pltpu
from jax.sharding import PartitionSpec as P

HEAD_DIM = 128
EPSILON = 1e-05
LOG2E = 1.4426950408889634
BLOCK = 256
COST = 0.05
MIB_FFN = 22
M_PROJ, M_OWN, M_EARLY, M_BWD, M_TIMES, M_BACK, M_BACKE, M_GRADS = 14, 16, 16, 20, 14, 24, 16, 18
f32, bf16 = jnp.float32, jnp.bfloat16
NN = ((1,), (0,))
NT = ((1,), (1,))
TN = ((0,), (0,))
ROW, GAIN_ONE, SHIFT_ONE, BIAS, B_OUT, GAIN_TWO, SHIFT_TWO, B_DOWN, B_UP = 0, 1, 2, 3, 6, 7, 8, 9, 10
SMEM = pl.BlockSpec(memory_space=pltpu.SMEM)


def dot(a, b, dims):
    return lax.dot_general(a, b, (dims, ((), ())), preferred_element_type=f32)


def ignoring(kernel, first, count):
    return lambda *refs: kernel(*refs[:first], *refs[first + count:])


def call(kernel, grid, in_specs, out_specs, out_shape, flops, moved, scratch=(), mib=20, aliases=None, deps=()):
    n = len(in_specs)
    run = pl.pallas_call(
        ignoring(kernel, n, len(deps)),
        grid=grid,
        in_specs=list(in_specs) + [pl.BlockSpec(memory_space=pl.ANY)] * len(deps),
        out_specs=out_specs,
        out_shape=out_shape,
        scratch_shapes=list(scratch),
        input_output_aliases=aliases or {},
        cost_estimate=pl.CostEstimate(flops=int(flops * COST), bytes_accessed=int(moved * COST), transcendentals=0),
        compiler_params=pltpu.CompilerParams(vmem_limit_bytes=mib * 2**20),
    )
    return lambda *args: run(*args, *deps)


def shape(dims, kind):
    return jax.ShapeDtypeStruct(dims, kind)


def near(dims, kind):
    return pltpu.VMEM(dims, kind)


def far(dims, kind):
    return pltpu.HBM(dims, kind)


def in_vmem(*arrays):
    return [pltpu.with_memory_space_constraint(a, pltpu.VMEM) for a in arrays]


def in_hbm(*arrays):
    return [pltpu.with_memory_space_constraint(a, pltpu.HBM) for a in arrays]


def whole(*dims):
    return pl.BlockSpec(dims, lambda *_: (0,) * len(dims), pipeline_mode=pl.Buffered(1))


def held(*dims):
    return pl.BlockSpec(dims, lambda *_: (0,) * len(dims))


def ln_parts(x):
    center = x - jnp.mean(x, axis=-1, keepdims=True)
    rstd = lax.rsqrt(jnp.mean(center * center, axis=-1, keepdims=True) + EPSILON)
    return center * rstd, rstd


def ln_back(grad, hat, rstd, gain):
    g = grad * gain
    return rstd * (g - jnp.mean(g, axis=-1, keepdims=True) - hat * jnp.mean(g * hat, axis=-1, keepdims=True))


def col_sum(a):
    return jnp.sum(a.astype(f32), axis=0, keepdims=True)


def project_kernel(first, x_ref, vec_ref, w_ref, normed_ref, out_ref):
    @pl.when(pl.program_id(0) == 0)
    def _():
        for i in range(x_ref.shape[0] // BLOCK):
            rows = slice(i * BLOCK, (i + 1) * BLOCK)
            hat, _ = ln_parts(x_ref[rows, :].astype(f32) + vec_ref[ROW:ROW + 1, :])
            normed_ref[rows, :] = (hat * vec_ref[GAIN_ONE:GAIN_ONE + 1, :] + vec_ref[SHIFT_ONE:SHIFT_ONE + 1, :]).astype(bf16)

    wide = w_ref.shape[1]
    at = first + pl.program_id(0) * wide
    lane = x_ref.shape[1]
    bias = vec_ref[pl.ds(BIAS + at // lane, 1), pl.ds(pl.multiple_of(at % lane, wide), wide)]
    out_ref[...] = (dot(normed_ref[...], w_ref[...], NN) + bias).astype(bf16)


def project(x, vectors, w, first, deps=()):
    T, D = x.shape
    wide = 512
    steps = (w.shape[1] - first) // wide
    skip = first // wide
    return call(
        functools.partial(project_kernel, first), (steps,),
        [whole(T, D), whole(*vectors.shape), pl.BlockSpec((D, wide), lambda c: (0, c + skip))],
        [held(T, D), pl.BlockSpec((T, wide), lambda c: (0, c))],
        [far((T, D), bf16), near((T, steps * wide), bf16)],
        2 * T * D * wide * steps, 10e6, deps=deps, mib=M_PROJ,
    )(x, vectors, *in_hbm(w))


def columns(first, h):
    return slice(first + h * HEAD_DIM, first + (h + 1) * HEAD_DIM)


def own_forward_kernel(j_ref, o_ref, lse_ref):
    T, D = o_ref.shape
    c = HEAD_DIM ** -0.5 * LOG2E
    row = lax.broadcasted_iota(jnp.int32, (BLOCK, BLOCK), 0)
    col = lax.broadcasted_iota(jnp.int32, (BLOCK, BLOCK), 1)
    for h in range(D // HEAD_DIM):
        head, k_head, v_head = (columns(i * D, h) for i in range(3))
        for i in range(T // BLOCK):
            rows = slice(i * BLOCK, (i + 1) * BLOCK)
            q = j_ref[rows, head]
            last = jnp.where(col <= row, dot(q, j_ref[rows, k_head], NT), -1e30)
            top = jnp.max(last, axis=1, keepdims=True)
            if i:
                s = dot(q, j_ref[:i * BLOCK, k_head], NT)
                top = jnp.maximum(top, jnp.max(s, axis=1, keepdims=True))
            top = top * c
            p = jnp.exp2(last * c - top)
            total = jnp.sum(p, axis=1, keepdims=True)
            o = dot(p.astype(bf16), j_ref[rows, v_head], NN)
            if i:
                p = jnp.exp2(s * c - top)
                total += jnp.sum(p, axis=1, keepdims=True)
                o += dot(p.astype(bf16), j_ref[:i * BLOCK, v_head], NN)
            o_ref[rows, head] = o / total
            lse_ref[rows, head] = jnp.broadcast_to(top + jnp.log2(total), (BLOCK, HEAD_DIM))


def early_forward_kernel(pos_ref, j_ref, e_ref, o1_ref, lse1_ref, att_ref, rest_ref, row_ref):
    T, D = att_ref.shape
    c = HEAD_DIM ** -0.5 * LOG2E
    shut = jnp.where(pos_ref[0] > 0, 0.0, -1e30).astype(f32)
    units = [(i, h) for h in range(D // HEAD_DIM) for i in range(T // BLOCK)]

    def scores(i, h):
        return dot(j_ref[i * BLOCK:(i + 1) * BLOCK, columns(0, h)], e_ref[:, columns(0, h)], NT)

    ahead = scores(*units[0])
    for n, (i, h) in enumerate(units):
        rows, head = slice(i * BLOCK, (i + 1) * BLOCK), columns(0, h)
        s = ahead
        if n + 1 < len(units):
            ahead = scores(*units[n + 1])
        top = jnp.max(s, axis=1, keepdims=True) * c
        p = jnp.exp2(s * c - top)
        total = jnp.sum(p, axis=1, keepdims=True)
        o2 = dot(p.astype(bf16), e_ref[:, columns(D, h)], NN) / total
        lse2 = jnp.broadcast_to(top + jnp.log2(total) + shut, (BLOCK, HEAD_DIM))
        lse1 = lse1_ref[rows, head]
        high = jnp.maximum(lse1, lse2)
        w1, w2 = jnp.exp2(lse1 - high), jnp.exp2(lse2 - high)
        both = w1 + w2
        o = (o1_ref[rows, head] * w1 + o2 * w2) / both
        low = o.astype(bf16)
        att_ref[rows, head] = low
        rest_ref[rows, head] = (o - low.astype(f32)).astype(bf16)
        row_ref[h, :, rows] = jnp.transpose(high + jnp.log2(both))[:8, :]


def all_of(*arrays):
    return [whole(*a.shape) for a in arrays]


def own_forward(joined, D):
    T = joined.shape[0]
    out = near((T, D), f32)
    return call(
        own_forward_kernel, (1,), all_of(joined), [whole(T, D)] * 2, [out, out], 12e9, 10e6, mib=M_OWN,
    )(*in_vmem(joined))


def early_forward(pos, joined, joined_e, o1, lse1):
    T, D = o1.shape
    H = D // HEAD_DIM
    return call(
        early_forward_kernel, (1,), [SMEM] + all_of(joined, joined_e, o1, lse1), [whole(T, D)] * 2 + [whole(H, 8, T)],
        [near((T, D), bf16), near((T, D), bf16), near((H, 8, T), f32)], 20e9, 12e6, mib=M_EARLY,
    )(pos, *in_vmem(joined, joined_e, o1, lse1))


def backward_kernel(causal, pos_ref, q_ref, k_ref, v_ref, do_ref, delta_ref, lse_ref, *refs):
    if causal:
        dq_in, out_ref, token_ref, dq_acc = refs
    else:
        dq_out, out_ref, token_ref, dq_acc = refs
    T, wide = q_ref.shape
    token_ref[...] = jnp.zeros(token_ref.shape, f32)
    scale = HEAD_DIM ** -0.5
    c = scale * LOG2E
    base = 1 if causal else 0
    key = lax.broadcasted_iota(jnp.int32, (BLOCK, BLOCK), 0)
    qry = lax.broadcasted_iota(jnp.int32, (BLOCK, BLOCK), 1)
    n = T // BLOCK
    many = wide // HEAD_DIM
    for h in range(many):
        head = columns(0, h)
        delta = delta_ref[pl.ds(pl.program_id(0) * many + h, 1), :]
        lse = lse_ref[h, :1, :]
        if not causal:
            lse = lse + jnp.where(pos_ref[0] > 0, 0.0, 1e30).astype(f32)
        for j in range(n):
            rows = slice(j * BLOCK, (j + 1) * BLOCK)
            a = j * BLOCK if causal else 0
            k = k_ref[rows, head]
            q = q_ref[a:, head]
            do = do_ref[a:, head]
            s = dot(k, q, NT)
            p = jnp.exp2(s * c - lse[:, a:])
            if causal:
                first = jnp.where(key <= qry, p[:, :BLOCK], 0.0)
                p = first if j == n - 1 else jnp.concatenate([first, p[:, BLOCK:]], axis=1)
            dp = dot(v_ref[rows, head], do, NT)
            ds = (p * (dp - delta[:, a:])).astype(bf16)
            out_ref[base + 1, rows, head] = dot(p.astype(bf16), do, NN).astype(bf16)
            out_ref[base, rows, head] = (dot(ds, q, NN) * scale).astype(bf16)
            part = jnp.transpose(dot(k, ds, TN))
            if j == 0:
                dq_acc[h] = part
            else:
                dq_acc[h, a:, :] += part
        dq = dq_acc[h] * scale
        if causal:
            out_ref[0, :, head] = (dq + dq_in[:, head]).astype(bf16)
        else:
            dq_out[:, head] = dq


MANY = 2


def backward_specs(T, D):
    H = D // HEAD_DIM
    spec = lambda skip=0: pl.BlockSpec((T, MANY * HEAD_DIM), lambda h: (0, h + skip * H // MANY))
    parts = lambda n: pl.BlockSpec((n, T, MANY * HEAD_DIM), lambda h: (0, 0, h))
    return H // MANY, spec, parts, [whole(H, T), pl.BlockSpec((MANY, 8, T), lambda h: (h, 0, 0))], [pltpu.VMEM((MANY, T, HEAD_DIM), f32)]


def early_backward(pos, joined, joined_e, do, delta, lse):
    T, D = do.shape
    steps, spec, parts, rows, scratch = backward_specs(T, D)
    return call(
        functools.partial(backward_kernel, False), (steps,), [SMEM, spec(), spec(), spec(1), spec()] + rows,
        [spec(), parts(2), held(8, HEAD_DIM)], [far((T, D), f32), near((2, T, D), bf16), shape((8, HEAD_DIM), f32)],
        26e9, 14e6, scratch, mib=M_BWD,
    )(pos, *in_hbm(joined, joined_e, joined_e, do), *in_vmem(delta, lse))


def own_backward(pos, joined, do, delta, lse, dq, deps=()):
    T, D = do.shape
    steps, spec, parts, rows, scratch = backward_specs(T, D)
    return call(
        functools.partial(backward_kernel, True), (steps,), [SMEM, spec(), spec(1), spec(2), spec()] + rows + [spec()],
        [parts(3), held(8, HEAD_DIM)], [near((3, T, D), bf16), shape((8, HEAD_DIM), f32)],
        22e9, 14e6, scratch, deps=deps, mib=M_BWD,
    )(pos, *in_hbm(joined, joined, joined, do), *in_vmem(delta, lse), *in_hbm(dq))


def ffn_kernel(x_ref, att_ref, rest_ref, vec_ref, g_ref, dact_ref, wo_ref, up_in, down_ref,
               out_ref, dmid_ref, datt_ref, branch_ref, n2_ref, act_ref, gup_ref, delta_ref, sums_ref, bup_sum_ref,
               up_ref, arrived):
    D, F, H = x_ref.shape[1], up_ref.shape[1], delta_ref.shape[0]

    first = pl.program_id(0) == 0
    copy = pltpu.make_async_copy(up_in, up_ref, arrived)

    @pl.when(first)
    def _():
        copy.start()
        sums_ref[...] = jnp.zeros(sums_ref.shape, f32)
        bup_sum_ref[...] = jnp.zeros(bup_sum_ref.shape, f32)

    vec = lambda i: vec_ref[i:i + 1, :]
    m = x_ref[...].astype(f32) + vec(ROW) + (dot(att_ref[...], wo_ref[...], NN) + vec(B_OUT))
    hat, rstd = ln_parts(m)
    n2_ref[...] = (hat * vec(GAIN_TWO) + vec(SHIFT_TWO)).astype(bf16)
    pl.when(first)(copy.wait)
    wide = 512
    for f in range(0, F, wide):
        cols = slice(f, f + wide)
        u = dot(n2_ref[...], up_ref[:, cols], NN) + vec(B_UP + f // D)[:, f % D:f % D + wide]
        d_act = dact_ref[:, cols].astype(f32)
        cdf = 0.5 * (1.0 + lax.erf(u * 0.7071067811865476))
        pdf = jnp.exp(-0.5 * u * u) * 0.3989422804014327
        act_ref[:, cols] = (u * cdf).astype(bf16)
        gup = (d_act * (cdf + u * pdf)).astype(bf16)
        gup_ref[:, cols] = gup
        bup_sum_ref[:, cols] += col_sum(gup)
    grad = dot(gup_ref[...], up_ref[...], NT)
    g = g_ref[...].astype(f32)
    d = g + ln_back(grad, hat, rstd, vec(GAIN_TWO))
    dmid_ref[...] = d
    low = d.astype(bf16)
    branch_ref[...] = low
    out_ref[...] = (m + (dot(act_ref[...], down_ref[...], NN) + vec(B_DOWN))).astype(bf16)
    datt = dot(low, wo_ref[...], NT).astype(bf16)
    datt_ref[...] = datt
    prod = datt.astype(f32) * (att_ref[...].astype(f32) + rest_ref[...].astype(f32))
    high = prod.astype(bf16)
    head = lax.broadcasted_iota(jnp.int32, (H, D), 0)
    heads = (lax.broadcasted_iota(jnp.int32, (H, D), 1) // HEAD_DIM == head).astype(bf16)
    delta_ref[...] = dot(heads, high, NT) + dot(heads, (prod - high.astype(f32)).astype(bf16), NT)
    for i, p in enumerate([col_sum(low), col_sum(grad * hat), col_sum(grad), col_sum(g)]):
        sums_ref[i:i + 1, :] += p


def ffn(x, att, rest, vectors, g, dact, wo, w_up, w_down):
    T, D = x.shape
    F = w_up.shape[1]
    H = D // HEAD_DIM
    part = lambda w: pl.BlockSpec((BLOCK, w), lambda i: (i, 0))
    return call(
        ffn_kernel, (T // BLOCK,),
        [part(D), part(D), part(D), whole(*vectors.shape), part(D), part(F), whole(D, D), pl.BlockSpec(memory_space=pltpu.HBM), whole(F, D)],
        [part(D)] * 5 + [part(F), part(F), pl.BlockSpec((H, BLOCK), lambda i: (0, i)), held(8, D), held(1, F)],
        [far((T, D), bf16), far((T, D), f32), far((T, D), bf16), near((T, D), bf16), near((T, D), bf16),
         near((T, F), bf16), near((T, F), bf16), near((H, T), f32), shape((8, D), f32), shape((1, F), f32)],
        2 * T * D * (2 * D + 4 * F) * 1.5, 30e6,
        [pltpu.VMEM((D, F), bf16), pltpu.SemaphoreType.DMA(())], mib=MIB_FFN,
    )(x, *in_vmem(att, rest), vectors, g, dact, *in_vmem(wo), *in_hbm(w_up), *in_vmem(w_down))


def times_kernel(a_ref, b_ref, out_ref):
    out_ref[...] = dot(a_ref[...], b_ref[...], NT).astype(bf16)


def times(a, b):
    T, D = a.shape
    F = b.shape[0]
    wide = 512
    return call(
        times_kernel, (F // wide,), [whole(T, D), pl.BlockSpec((wide, D), lambda f: (f, 0))], pl.BlockSpec((T, wide), lambda f: (0, f)),
        far((T, F), bf16), 2 * T * D * F, 8e6, mib=M_TIMES,
    )(*in_hbm(a, b))


def grads_kernel(rows, terms, lefts, core_ref, place_ref, *refs):
    left, refs = refs[:lefts], refs[lefts:]
    mine_ref, theirs_ref, acc = refs[-3:]
    core = core_ref[0]
    first = pl.program_id(0) * (acc.shape[0] // 2)
    lane = mine_ref.shape[2]
    at = base = 0
    for group in terms:
        total = None
        for a, part in group:
            b = refs[at][part] if len(refs[at].shape) == 3 else refs[at][...]
            at += 1
            add = dot(left[a][...], b, TN)
            total = add if total is None else total + add
        acc[...] = total.reshape(acc.shape)
        for h in range(acc.shape[2] // lane):
            cols = slice(h * lane, (h + 1) * lane)
            for i in range(acc.shape[0] // 2):
                own = place_ref[core, first + i]
                other = place_ref[1 - core, first + i]
                mine_ref[own, base:base + rows, :] = acc[2 * i + core, :, cols].astype(bf16)
                theirs_ref[other, base:base + rows, :] = acc[2 * i + 1 - core, :, cols].astype(bf16)
            base += rows


def grads(core, place, lefts, terms, devices, total_rows, row_block, block_rows, into=None, deps=()):
    T, R = lefts[0].shape
    rows = R // devices
    steps = 4
    lane = 1024
    flat = [term for group in terms for term in group]
    ins = [core, place] + list(lefts)
    specs = [SMEM, SMEM] + [pl.BlockSpec((T, R // steps), lambda s: (0, s))] * len(lefts)
    for _, array, part in flat:
        ins.extend(in_vmem(array))
        specs.append(whole(*array.shape))
    aliases = {}
    if into is not None:
        aliases = {len(ins): 0, len(ins) + 1: 1}
        ins += list(into)
        specs += [pl.BlockSpec(memory_space=pl.ANY)] * 2
    kernel = functools.partial(grads_kernel, rows, [[(a, part) for a, _, part in group] for group in terms], len(lefts))
    width = flat[0][1].shape[-1]
    block = pl.BlockSpec((devices // 2, block_rows, lane), lambda s: (0, row_block, 0))
    out = far((devices // 2, total_rows, lane), bf16)
    return call(
        kernel, (steps,), specs, [block, block], [out, out], 3 * T * R * width * len(flat), 20e6,
        [pltpu.VMEM((devices // steps, rows, width), f32)], aliases=aliases, deps=deps, mib=M_GRADS,
    )(*ins)


def plain_grads(lefts, terms, devices):
    out = []
    for group in terms:
        total = sum(dot(lefts[a], b if b.ndim == 2 else b[p], TN) for a, b, p in group).astype(bf16)
        lane = 1024
        split = total.reshape(devices, -1, total.shape[1] // lane, lane).transpose(0, 2, 1, 3)
        out.append(split.reshape(devices, -1, lane))
    return jnp.concatenate(out, axis=1)


def back_kernel(own, first, x_ref, vec_ref, dj_ref, w_in, *refs):
    if own:
        dmid_ref, out_ref, sums_ref, w_ref, arrived = refs
    else:
        out_ref, sums_ref = refs
    D = x_ref.shape[1]
    n = dj_ref.shape[0]
    start = pl.program_id(0) == 0
    copies = [pltpu.make_async_copy(w_in.at[:, i * D:(i + 1) * D], w_ref.at[i], arrived.at[i]) for i in range(n)] if own else []

    @pl.when(start)
    def _():
        for copy in copies:
            copy.start()
        sums_ref[...] = jnp.zeros(sums_ref.shape, f32)

    hat, rstd = ln_parts(x_ref[...].astype(f32) + vec_ref[ROW:ROW + 1, :])
    grad = None
    for i in range(n):
        if own:
            pl.when(start)(copies[i].wait)
            w = w_ref[i]
        else:
            w = w_in[:, first + i * D:first + (i + 1) * D]
        part = dot(dj_ref[i], w, NT)
        grad = part if grad is None else grad + part
    d = ln_back(grad, hat, rstd, vec_ref[GAIN_ONE:GAIN_ONE + 1, :])
    if own:
        d = d + dmid_ref[...]
    out_ref[...] = d.astype(out_ref.dtype)
    sums = [col_sum(d), col_sum(grad * hat), col_sum(grad), col_sum(dj_ref[n - 1])]
    if own:
        sums.append(col_sum(dj_ref[0]))
    for i, p in enumerate(sums):
        sums_ref[i:i + 1, :] += p


def back(x, vectors, dj, w, first, dmid=None, deps=()):
    T, D = x.shape
    n = dj.shape[0]
    own = dmid is not None
    part = pl.BlockSpec((BLOCK, D), lambda i: (i, 0))
    ins = [*in_hbm(x), vectors, *in_hbm(dj, w), *in_hbm(dmid)] if own else [x, vectors, *in_vmem(dj, w)]
    specs = [part, whole(*vectors.shape), pl.BlockSpec((n, BLOCK, D), lambda i: (0, i, 0)),
             pl.BlockSpec(memory_space=pltpu.HBM) if own else whole(*w.shape)]
    return call(
        functools.partial(back_kernel, own, first), (T // BLOCK,), specs + ([part] if own else []), [part, held(8, D)],
        [far((T, D), f32 if own else bf16), shape((8, D), f32)],
        2 * T * D * n * D * 1.5, 16e6, [pltpu.VMEM((n, D, D), bf16), pltpu.SemaphoreType.DMA((n,))] if own else [], deps=deps, mib=M_BACK if own else M_BACKE,
    )(*ins)


class Scatter:
    def __init__(self, mesh, x_first):
        self.seq, self.dp = mesh.shape["seq"], mesh.shape["dp"]
        bits = []
        step = 2
        while step < self.dp:
            bits.append(step)
            step *= 2
        if x_first:
            self.orders = [[0] + bits, bits + [0]]
        else:
            self.orders = [bits + [0], [bits[1], bits[0], 0] + bits[2:]]
        self.stages = len(bits) + 1
        self.count = 1 << self.stages

    def block(self, core, place):
        s, d = 0, core
        for k, bit in enumerate(self.orders[core]):
            on = (place >> (self.stages - 1 - k)) & 1
            if bit == 0:
                s = on
            else:
                d += bit * on
        return s * self.dp + d

    def places(self):
        table = [[0] * self.count for _ in range(2)]
        for c in range(2):
            for p in range(self.count):
                table[c][self.block(c, p) // 2] = p
        return jnp.array(table, jnp.int32)

    def mine_theirs(self, grad):
        core = lax.axis_index("dp") % 2
        pick = [grad[jnp.array([self.block(c, p) for p in range(self.count)])] for c in range(2)]
        return jnp.where(core == 0, pick[0], pick[1]), jnp.where(core == 0, pick[1], pick[0])

    def begin(self, mine, theirs):
        got = lax.ppermute(theirs, "dp", [(i, i ^ 1) for i in range(self.dp)])
        return [mine, got], [0, 0], self.count

    def pairs(self, k):
        pairs = []
        for a in range(self.seq):
            for b in range(self.dp):
                bit = self.orders[b % 2][k]
                to = ((1 - a) * self.dp + b) if bit == 0 else (a * self.dp + (b ^ bit))
                pairs.append((a * self.dp + b, to))
        return pairs

    def total(self, state, at, size):
        arrays, bases, _ = state
        return sum(lax.dynamic_slice_in_dim(a, base + at, size, 0).astype(f32) for a, base in zip(arrays, bases))

    def step(self, k, state, beside=None):
        d = lax.axis_index("dp")
        core = d % 2
        own = [lax.axis_index("seq") if o[k] == 0 else (d // o[k]) % 2 for o in self.orders]
        own = jnp.where(core == 0, own[0], own[1])
        arrays, bases, size = state
        half = size // 2
        send = self.total(state, (1 - own) * half, half).astype(bf16)
        if beside is not None:
            send, beside = lax.optimization_barrier((send, beside))
        got = lax.ppermute(send, ("seq", "dp"), self.pairs(k))
        return (arrays + [got], [base + own * half for base in bases] + [0], half), send if beside is None else beside

    def finish(self, first, state):
        for k in range(first, self.stages):
            state, _ = self.step(k, state)
        return self.total(state, 0, 1)[0]


def tie(state, *others):
    arrays, bases, size = state
    out = lax.optimization_barrier(tuple(arrays) + others)
    return (list(out[:len(arrays)]), bases, size), out[len(arrays):]


def make_local(mesh):
    scatter, scatter_b = Scatter(mesh, False), Scatter(mesh, True)
    devices = scatter.seq * scatter.dp

    def local(tokens, domain, domain_table, gain_one, shift_one, wqkv, bias_q, bias_v, w_out, b_out,
              gain_two, shift_two, w_up, b_up, w_down, b_down, cotangent):
        _, T, D = tokens.shape
        F = w_up.shape[1]
        share, ff = D // devices, F // devices
        kernels = share % 16 == 0
        line = [domain_table[domain[0]], gain_one, shift_one, bias_q, None, bias_v, b_out, gain_two, shift_two, b_down]
        line += [b_up[i:i + D] for i in range(0, F, D)]
        at = lax.broadcasted_iota(jnp.int32, (16, D), 0)
        vectors = jnp.zeros((16, D), f32)
        for i, v in enumerate(line):
            if v is not None:
                vectors = jnp.where(at == i, v.astype(f32)[None, :], vectors)
        pos = lax.axis_index("seq").astype(jnp.int32)[None]
        core = (lax.axis_index("dp") % 2).astype(jnp.int32)[None]
        place, place_b = scatter.places(), scatter_b.places()
        x, g = tokens[0], cotangent[0]
        early_x = lax.ppermute(x, "seq", [(0, 1)])

        normed, joined = project(x, vectors, wqkv, 0)
        o1, lse1 = own_forward(joined, D)
        d_act = times(g, w_down)
        normed_e, joined_e = project(early_x, vectors, wqkv, D, [d_act, o1])
        attended, rest, lse = early_forward(pos, joined, joined_e, o1, lse1)
        output, d_mid, d_att, branch, n2, active, g_upper, delta, sums_two, bup_sum = ffn(
            x, attended, rest, vectors, g, d_act, w_out, w_up, w_down)
        rows_a = ff + 2 * share + share
        if kernels:
            a = grads(core, place, [active], [[(0, g, 0)]], devices, rows_a, 0, ff)
            a = grads(core, place, [n2], [[(0, g_upper, 0)]], devices, rows_a, ff // (2 * share), 2 * share, into=a)
            a = grads(core, place, [attended], [[(0, branch, 0)]], devices, rows_a, (ff + 2 * share) // share, share, into=a)
        else:
            a = scatter.mine_theirs(jnp.concatenate([
                plain_grads([active], [[(0, g, 0)]], devices),
                plain_grads([n2], [[(0, g_upper, 0)]], devices),
                plain_grads([attended], [[(0, branch, 0)]], devices)], axis=1))
        a = scatter.begin(*a)
        dq_e, dj_e, token = early_backward(pos, joined, joined_e, d_att, delta, lse)
        a, (token,) = tie(a, token)
        a, sent = scatter.step(0, a)
        dln_e, sums_e = back(early_x, vectors, dj_e, wqkv, D, None, [sent, token])
        from_late = lax.ppermute(dln_e, "seq", [(1, 0)])
        dj, token = own_backward(pos, joined, d_att, delta, lse, dq_e, [dln_e])
        a, (token,) = tie(a, token)
        a, sent = scatter.step(1, a)
        terms = [[(0, dj, 0)], [(0, dj, 1), (1, dj_e, 0)], [(0, dj, 2), (1, dj_e, 1)]]
        if kernels:
            b = grads(core, place_b, in_hbm(normed, normed_e), terms, devices, 3 * share, 0, 3 * share, deps=[sent, token])
        else:
            b = scatter_b.mine_theirs(plain_grads([normed, normed_e], terms, devices))
        a, (from_late, *b) = tie(a, from_late, *b)
        a, theirs = scatter.step(2, a, b[1])
        b = scatter_b.begin(b[0], theirs)
        b, sent = scatter_b.step(0, b)
        base, sums_one = back(x, vectors, dj, wqkv, 0, d_mid, [sent])
        b, (base,) = tie(b, base)
        sums_one = jnp.concatenate([sums_one[:4] + sums_e[:4], sums_one[4:5]], axis=0)
        domains = domain_table.shape[0]
        onehot = (jnp.arange(domains, dtype=jnp.int32) == domain[0]).astype(f32)
        small = jnp.concatenate([
            onehot[:, None] * sums_one[:1], sums_one[1:3], sums_one[4:5], sums_one[3:4], sums_two[:4]], axis=0)
        small = small.reshape(-1, devices, share).transpose(1, 0, 2).reshape(devices, -1)
        small = jnp.concatenate([small, bup_sum.reshape(devices, -1)], axis=1)
        b, small = scatter_b.step(1, b, small)
        a, (base,) = tie(a, base)
        a, _ = scatter.step(3, a)
        flat = jnp.sum(lax.all_to_all(small, ("seq", "dp"), 0, 0, tiled=True), axis=0)
        b, flat = scatter_b.step(2, b, flat)
        a, (flat,) = tie(a, flat)
        grad_tokens = (base + from_late.astype(f32)).astype(bf16)
        b, (grad_tokens,) = tie(b, grad_tokens)
        sum_b = scatter_b.finish(3, b)
        sum_a = scatter.finish(4, a)

        join = lambda a, n: jnp.concatenate([a[i * share:(i + 1) * share] for i in range(n)], axis=1)
        piece = lambda i: flat[i * share:(i + 1) * share]
        m = domains
        return (
            output[None], grad_tokens[None], flat[:m * share].reshape(m, share), piece(m), piece(m + 1), join(sum_b, 3),
            piece(m + 2), piece(m + 3), sum_a[ff + 2 * share:], piece(m + 4), piece(m + 5), piece(m + 6),
            join(sum_a[ff:], 2), flat[(m + 8) * share:(m + 8) * share + ff], sum_a[:ff], piece(m + 7))

    return local


def solution(mesh):
    both = ("seq", "dp")
    lead, rows = P("dp", "seq", None), P(both, None)
    return jax.shard_map(
        make_local(mesh),
        mesh=mesh,
        in_specs=(lead, P("dp")) + (P(),) * 14 + (lead,),
        out_specs=(lead, lead, P(None, both), P(both), P(both), rows, P(both), P(both), rows, P(both), P(both), P(both),
                   rows, P(both), rows, P(both)),
        check_vma=False,
    )
```

```python
import functools

import jax
import jax.numpy as jnp
from jax import lax
from jax.experimental import pallas as pl
from jax.experimental.pallas import tpu as pltpu
from jax.sharding import PartitionSpec as P

HEAD_DIM = 128
EPSILON = 1e-05
LOG2E = 1.4426950408889634
BLOCK = 256
COST = 0.05
MIB_FFN = 22
M_PROJ, M_OWN, M_EARLY, M_BWD, M_TIMES, M_BACK, M_BACKE, M_GRADS = 14, 16, 16, 30, 14, 24, 16, 18
f32, bf16 = jnp.float32, jnp.bfloat16
NN = ((1,), (0,))
NT = ((1,), (1,))
TN = ((0,), (0,))
ROW, GAIN_ONE, SHIFT_ONE, BIAS, B_OUT, GAIN_TWO, SHIFT_TWO, B_DOWN, B_UP = 0, 1, 2, 3, 6, 7, 8, 9, 10
SMEM = pl.BlockSpec(memory_space=pltpu.SMEM)


def dot(a, b, dims):
    return lax.dot_general(a, b, (dims, ((), ())), preferred_element_type=f32)


def ignoring(kernel, first, count):
    return lambda *refs: kernel(*refs[:first], *refs[first + count:])


def call(kernel, grid, in_specs, out_specs, out_shape, flops, moved, scratch=(), mib=20, aliases=None, deps=()):
    n = len(in_specs)
    run = pl.pallas_call(
        ignoring(kernel, n, len(deps)),
        grid=grid,
        in_specs=list(in_specs) + [pl.BlockSpec(memory_space=pl.ANY)] * len(deps),
        out_specs=out_specs,
        out_shape=out_shape,
        scratch_shapes=list(scratch),
        input_output_aliases=aliases or {},
        cost_estimate=pl.CostEstimate(flops=int(flops * COST), bytes_accessed=int(moved * COST), transcendentals=0),
        compiler_params=pltpu.CompilerParams(vmem_limit_bytes=mib * 2**20),
    )
    return lambda *args: run(*args, *deps)


def shape(dims, kind):
    return jax.ShapeDtypeStruct(dims, kind)


def near(dims, kind):
    return pltpu.VMEM(dims, kind)


def far(dims, kind):
    return pltpu.HBM(dims, kind)


def in_vmem(*arrays):
    return [pltpu.with_memory_space_constraint(a, pltpu.VMEM) for a in arrays]


def in_hbm(*arrays):
    return [pltpu.with_memory_space_constraint(a, pltpu.HBM) for a in arrays]


def whole(*dims):
    return pl.BlockSpec(dims, lambda *_: (0,) * len(dims), pipeline_mode=pl.Buffered(1))


def held(*dims):
    return pl.BlockSpec(dims, lambda *_: (0,) * len(dims))


def ln_parts(x):
    center = x - jnp.mean(x, axis=-1, keepdims=True)
    rstd = lax.rsqrt(jnp.mean(center * center, axis=-1, keepdims=True) + EPSILON)
    return center * rstd, rstd


def ln_back(grad, hat, rstd, gain):
    g = grad * gain
    return rstd * (g - jnp.mean(g, axis=-1, keepdims=True) - hat * jnp.mean(g * hat, axis=-1, keepdims=True))


def col_sum(a):
    return jnp.sum(a.astype(f32), axis=0, keepdims=True)


def project_kernel(first, x_ref, vec_ref, w_ref, normed_ref, out_ref):
    @pl.when(pl.program_id(0) == 0)
    def _():
        for i in range(x_ref.shape[0] // BLOCK):
            rows = slice(i * BLOCK, (i + 1) * BLOCK)
            hat, _ = ln_parts(x_ref[rows, :].astype(f32) + vec_ref[ROW:ROW + 1, :])
            normed_ref[rows, :] = (hat * vec_ref[GAIN_ONE:GAIN_ONE + 1, :] + vec_ref[SHIFT_ONE:SHIFT_ONE + 1, :]).astype(bf16)

    wide = w_ref.shape[1]
    at = first + pl.program_id(0) * wide
    lane = x_ref.shape[1]
    bias = vec_ref[pl.ds(BIAS + at // lane, 1), pl.ds(pl.multiple_of(at % lane, wide), wide)]
    out_ref[...] = (dot(normed_ref[...], w_ref[...], NN) + bias).astype(bf16)


def project(x, vectors, w, first, deps=()):
    T, D = x.shape
    wide = 512
    steps = (w.shape[1] - first) // wide
    skip = first // wide
    return call(
        functools.partial(project_kernel, first), (steps,),
        [whole(T, D), whole(*vectors.shape), pl.BlockSpec((D, wide), lambda c: (0, c + skip))],
        [held(T, D), pl.BlockSpec((T, wide), lambda c: (0, c))],
        [far((T, D), bf16), near((T, steps * wide), bf16)],
        2 * T * D * wide * steps, 10e6, deps=deps, mib=M_PROJ,
    )(x, vectors, *in_hbm(w))


def columns(first, h):
    if isinstance(h, int):
        return slice(first + h * HEAD_DIM, first + (h + 1) * HEAD_DIM)
    return pl.ds(pl.multiple_of(first + h * HEAD_DIM, HEAD_DIM), HEAD_DIM)


def own_forward_kernel(j_ref, o_ref, lse_ref):
    T, D = o_ref.shape
    c = HEAD_DIM ** -0.5 * LOG2E
    row = lax.broadcasted_iota(jnp.int32, (BLOCK, BLOCK), 0)
    col = lax.broadcasted_iota(jnp.int32, (BLOCK, BLOCK), 1)
    for pair in range(2):
        h = pl.program_id(0) * 2 + pair
        head, k_head, v_head = (columns(i * D, h) for i in range(3))
        for i in range(T // BLOCK):
            rows = slice(i * BLOCK, (i + 1) * BLOCK)
            q = j_ref[rows, head]
            last = jnp.where(col <= row, dot(q, j_ref[rows, k_head], NT), -1e30)
            top = jnp.max(last, axis=1, keepdims=True)
            if i:
                s = dot(q, j_ref[:i * BLOCK, k_head], NT)
                top = jnp.maximum(top, jnp.max(s, axis=1, keepdims=True))
            top = top * c
            p = jnp.exp2(last * c - top)
            total = jnp.sum(p, axis=1, keepdims=True)
            o = dot(p.astype(bf16), j_ref[rows, v_head], NN)
            if i:
                p = jnp.exp2(s * c - top)
                total += jnp.sum(p, axis=1, keepdims=True)
                o += dot(p.astype(bf16), j_ref[:i * BLOCK, v_head], NN)
            o_ref[rows, head] = o / total
            lse_ref[rows, head] = jnp.broadcast_to(top + jnp.log2(total), (BLOCK, HEAD_DIM))


def early_forward_kernel(pos_ref, j_ref, e_ref, o1_ref, lse1_ref, att_ref, rest_ref, row_ref):
    T, D = att_ref.shape
    c = HEAD_DIM ** -0.5 * LOG2E
    shut = jnp.where(pos_ref[0] > 0, 0.0, -1e30).astype(f32)
    units = [(i, pl.program_id(0) * 2 + pair) for pair in range(2) for i in range(T // BLOCK)]

    def scores(i, h):
        return dot(j_ref[i * BLOCK:(i + 1) * BLOCK, columns(0, h)], e_ref[:, columns(0, h)], NT)

    ahead = scores(*units[0])
    for n, (i, h) in enumerate(units):
        rows, head = slice(i * BLOCK, (i + 1) * BLOCK), columns(0, h)
        s = ahead
        if n + 1 < len(units):
            ahead = scores(*units[n + 1])
        top = jnp.max(s, axis=1, keepdims=True) * c
        p = jnp.exp2(s * c - top)
        total = jnp.sum(p, axis=1, keepdims=True)
        o2 = dot(p.astype(bf16), e_ref[:, columns(D, h)], NN) / total
        lse2 = jnp.broadcast_to(top + jnp.log2(total) + shut, (BLOCK, HEAD_DIM))
        lse1 = lse1_ref[rows, head]
        high = jnp.maximum(lse1, lse2)
        w1, w2 = jnp.exp2(lse1 - high), jnp.exp2(lse2 - high)
        both = w1 + w2
        o = (o1_ref[rows, head] * w1 + o2 * w2) / both
        low = o.astype(bf16)
        att_ref[rows, head] = low
        rest_ref[rows, head] = (o - low.astype(f32)).astype(bf16)
        row_ref[h, :, rows] = jnp.transpose(high + jnp.log2(both))[:8, :]


def all_of(*arrays):
    return [whole(*a.shape) for a in arrays]


def own_forward(joined, D):
    T = joined.shape[0]
    out = near((T, D), f32)
    return call(
        own_forward_kernel, (D // HEAD_DIM // 2,), all_of(joined), [whole(T, D)] * 2, [out, out], 12e9, 10e6, mib=M_OWN,
    )(*in_vmem(joined))


def early_forward(pos, joined, joined_e, o1, lse1):
    T, D = o1.shape
    H = D // HEAD_DIM
    return call(
        early_forward_kernel, (H // 2,), [SMEM] + all_of(joined, joined_e, o1, lse1), [whole(T, D)] * 2 + [whole(H, 8, T)],
        [near((T, D), bf16), near((T, D), bf16), near((H, 8, T), f32)], 20e9, 12e6, mib=M_EARLY,
    )(pos, *in_vmem(joined, joined_e, o1, lse1))


def backward_kernel(causal, pos_ref, q_ref, k_ref, v_ref, do_ref, delta_ref, lse_ref, *refs):
    if causal:
        dq_in, out_ref, token_ref, dq_acc = refs
    else:
        dq_out, out_ref, token_ref, dq_acc = refs
    T, wide = q_ref.shape
    token_ref[...] = jnp.zeros(token_ref.shape, f32)
    scale = HEAD_DIM ** -0.5
    c = scale * LOG2E
    base = 1 if causal else 0
    key = lax.broadcasted_iota(jnp.int32, (BLOCK, BLOCK), 0)
    qry = lax.broadcasted_iota(jnp.int32, (BLOCK, BLOCK), 1)
    n = T // BLOCK
    many = wide // HEAD_DIM
    for h in range(many):
        head = columns(0, h)
        delta = delta_ref[pl.ds(pl.program_id(0) * many + h, 1), :]
        lse = lse_ref[h, :1, :]
        if not causal:
            lse = lse + jnp.where(pos_ref[0] > 0, 0.0, 1e30).astype(f32)
        for j in range(n):
            rows = slice(j * BLOCK, (j + 1) * BLOCK)
            a = j * BLOCK if causal else 0
            k = k_ref[rows, head]
            q = q_ref[a:, head]
            do = do_ref[a:, head]
            s = dot(k, q, NT)
            p = jnp.exp2(s * c - lse[:, a:])
            if causal:
                first = jnp.where(key <= qry, p[:, :BLOCK], 0.0)
                p = first if j == n - 1 else jnp.concatenate([first, p[:, BLOCK:]], axis=1)
            dp = dot(v_ref[rows, head], do, NT)
            ds = (p * (dp - delta[:, a:])).astype(bf16)
            out_ref[base + 1, rows, head] = dot(p.astype(bf16), do, NN).astype(bf16)
            out_ref[base, rows, head] = (dot(ds, q, NN) * scale).astype(bf16)
            part = jnp.transpose(dot(k, ds, TN))
            if j == 0:
                dq_acc[h] = part
            else:
                dq_acc[h, a:, :] += part
        dq = dq_acc[h] * scale
        if causal:
            out_ref[0, :, head] = (dq + dq_in[:, head]).astype(bf16)
        else:
            dq_out[:, head] = dq


MANY = 4


def backward_specs(T, D):
    H = D // HEAD_DIM
    spec = lambda skip=0: pl.BlockSpec((T, MANY * HEAD_DIM), lambda h: (0, h + skip * H // MANY))
    parts = lambda n: pl.BlockSpec((n, T, MANY * HEAD_DIM), lambda h: (0, 0, h))
    return H // MANY, spec, parts, [whole(H, T), pl.BlockSpec((MANY, 8, T), lambda h: (h, 0, 0))], [pltpu.VMEM((MANY, T, HEAD_DIM), f32)]


def early_backward(pos, joined, joined_e, do, delta, lse):
    T, D = do.shape
    steps, spec, parts, rows, scratch = backward_specs(T, D)
    return call(
        functools.partial(backward_kernel, False), (steps,), [SMEM, spec(), spec(), spec(1), spec()] + rows,
        [spec(), parts(2), held(8, HEAD_DIM)], [far((T, D), f32), near((2, T, D), bf16), shape((8, HEAD_DIM), f32)],
        26e9, 14e6, scratch, mib=M_BWD,
    )(pos, *in_hbm(joined, joined_e, joined_e, do), *in_vmem(delta, lse))


def own_backward(pos, joined, do, delta, lse, dq, deps=()):
    T, D = do.shape
    steps, spec, parts, rows, scratch = backward_specs(T, D)
    return call(
        functools.partial(backward_kernel, True), (steps,), [SMEM, spec(), spec(1), spec(2), spec()] + rows + [spec()],
        [parts(3), held(8, HEAD_DIM)], [near((3, T, D), bf16), shape((8, HEAD_DIM), f32)],
        22e9, 14e6, scratch, deps=deps, mib=M_BWD,
    )(pos, *in_hbm(joined, joined, joined, do), *in_vmem(delta, lse), *in_hbm(dq))


def ffn_kernel(x_ref, att_ref, rest_ref, vec_ref, g_ref, dact_ref, wo_ref, up_in, down_ref,
               out_ref, dmid_ref, datt_ref, branch_ref, n2_ref, act_ref, gup_ref, delta_ref, sums_ref, bup_sum_ref,
               up_ref, arrived):
    D, F, H = x_ref.shape[1], up_ref.shape[1], delta_ref.shape[0]

    first = pl.program_id(0) == 0
    copy = pltpu.make_async_copy(up_in, up_ref, arrived)

    @pl.when(first)
    def _():
        copy.start()
        sums_ref[...] = jnp.zeros(sums_ref.shape, f32)
        bup_sum_ref[...] = jnp.zeros(bup_sum_ref.shape, f32)

    vec = lambda i: vec_ref[i:i + 1, :]
    m = x_ref[...].astype(f32) + vec(ROW) + (dot(att_ref[...], wo_ref[...], NN) + vec(B_OUT))
    hat, rstd = ln_parts(m)
    n2_ref[...] = (hat * vec(GAIN_TWO) + vec(SHIFT_TWO)).astype(bf16)
    pl.when(first)(copy.wait)
    wide = 512
    for f in range(0, F, wide):
        cols = slice(f, f + wide)
        u = dot(n2_ref[...], up_ref[:, cols], NN) + vec(B_UP + f // D)[:, f % D:f % D + wide]
        d_act = dact_ref[:, cols].astype(f32)
        cdf = 0.5 * (1.0 + lax.erf(u * 0.7071067811865476))
        pdf = jnp.exp(-0.5 * u * u) * 0.3989422804014327
        act_ref[:, cols] = (u * cdf).astype(bf16)
        gup = (d_act * (cdf + u * pdf)).astype(bf16)
        gup_ref[:, cols] = gup
        bup_sum_ref[:, cols] += col_sum(gup)
    grad = dot(gup_ref[...], up_ref[...], NT)
    g = g_ref[...].astype(f32)
    d = g + ln_back(grad, hat, rstd, vec(GAIN_TWO))
    dmid_ref[...] = d
    low = d.astype(bf16)
    branch_ref[...] = low
    out_ref[...] = (m + (dot(act_ref[...], down_ref[...], NN) + vec(B_DOWN))).astype(bf16)
    datt = dot(low, wo_ref[...], NT).astype(bf16)
    datt_ref[...] = datt
    prod = datt.astype(f32) * (att_ref[...].astype(f32) + rest_ref[...].astype(f32))
    high = prod.astype(bf16)
    head = lax.broadcasted_iota(jnp.int32, (H, D), 0)
    heads = (lax.broadcasted_iota(jnp.int32, (H, D), 1) // HEAD_DIM == head).astype(bf16)
    delta_ref[...] = dot(heads, high, NT) + dot(heads, (prod - high.astype(f32)).astype(bf16), NT)
    for i, p in enumerate([col_sum(low), col_sum(grad * hat), col_sum(grad), col_sum(g)]):
        sums_ref[i:i + 1, :] += p


def ffn(x, att, rest, vectors, g, dact, wo, w_up, w_down):
    T, D = x.shape
    F = w_up.shape[1]
    H = D // HEAD_DIM
    part = lambda w: pl.BlockSpec((BLOCK, w), lambda i: (i, 0))
    return call(
        ffn_kernel, (T // BLOCK,),
        [part(D), part(D), part(D), whole(*vectors.shape), part(D), part(F), whole(D, D), pl.BlockSpec(memory_space=pltpu.HBM), whole(F, D)],
        [part(D)] * 5 + [part(F), part(F), pl.BlockSpec((H, BLOCK), lambda i: (0, i)), held(8, D), held(1, F)],
        [far((T, D), bf16), far((T, D), f32), far((T, D), bf16), near((T, D), bf16), near((T, D), bf16),
         near((T, F), bf16), near((T, F), bf16), near((H, T), f32), shape((8, D), f32), shape((1, F), f32)],
        2 * T * D * (2 * D + 4 * F) * 1.5, 30e6,
        [pltpu.VMEM((D, F), bf16), pltpu.SemaphoreType.DMA(())], mib=MIB_FFN,
    )(x, *in_vmem(att, rest), vectors, g, dact, *in_vmem(wo), *in_hbm(w_up), *in_vmem(w_down))


def times_kernel(a_ref, b_ref, out_ref):
    out_ref[...] = dot(a_ref[...], b_ref[...], NT).astype(bf16)


def times(a, b):
    T, D = a.shape
    F = b.shape[0]
    wide = 512
    return call(
        times_kernel, (F // wide,), [whole(T, D), pl.BlockSpec((wide, D), lambda f: (f, 0))], pl.BlockSpec((T, wide), lambda f: (0, f)),
        far((T, F), bf16), 2 * T * D * F, 8e6, mib=M_TIMES,
    )(*in_hbm(a, b))


def grads_kernel(parts, lefts, rights, core_ref, place_ref, *refs):
    left, right = refs[:lefts], refs[lefts:lefts + rights]
    mine_ref, theirs_ref, stage, sent = refs[lefts + rights:]
    core = core_ref[0]
    shards, lane = stage.shape[1], stage.shape[3]
    step = pl.program_id(0)

    def copies(at):
        for i in range(shards // 2):
            for n, (out_ref, kind) in enumerate(((mine_ref, core), (theirs_ref, 1 - core))):
                yield pltpu.make_async_copy(
                    stage.at[at % 2, 2 * i + kind], out_ref.at[place_ref[kind, at * (shards // 2) + i]], sent.at[at % 2, 2 * i + n])

    def wait(at):
        for copy in copies(at):
            copy.wait()

    pl.when(step >= 2)(functools.partial(wait, step - 2))
    for terms, rows, base in parts:
        total = None
        for a, b, sub in terms:
            add = dot(left[a][...], right[b][...] if sub is None else right[b][sub], TN)
            total = add if total is None else total + add
        for h in range(total.shape[1] // lane):
            first = base + h * rows
            stage[step % 2, :, first:first + rows, :] = total[:, h * lane:(h + 1) * lane].reshape(shards, rows, lane).astype(bf16)
    for copy in copies(step):
        copy.start()

    @pl.when(step == pl.num_programs(0) - 1)
    def _():
        wait(step - 1)
        wait(step)


def grads(core, place, lefts, rights, parts, devices, deps=()):
    T = lefts[0].shape[0]
    steps, lane = 4, 1024
    shards = devices // steps
    height = sum(rows * rights[terms[0][1]].shape[-1] // lane for terms, rows, _ in parts)
    ins = list(lefts) + in_vmem(*rights)
    out = far((devices // 2, height, lane), bf16)
    flops = sum(2 * T * rows * devices * rights[b].shape[-1] for terms, rows, _ in parts for _, b, _ in terms)
    hbm = pl.BlockSpec(memory_space=pltpu.HBM)
    return call(
        functools.partial(grads_kernel, parts, len(lefts), len(rights)), (steps,),
        [SMEM, SMEM] + [pl.BlockSpec((T, a.shape[1] // steps), lambda s: (0, s)) for a in lefts] + all_of(*rights), [hbm, hbm], [out, out],
        1.5 * flops, 20e6, [pltpu.VMEM((2, shards, height, lane), bf16), pltpu.SemaphoreType.DMA((2, shards))],
        deps=deps, mib=M_GRADS,
    )(core, place, *ins)


def plain_grads(lefts, terms, devices):
    out = []
    for group in terms:
        total = sum(dot(lefts[a], b if b.ndim == 2 else b[p], TN) for a, b, p in group).astype(bf16)
        lane = 1024
        split = total.reshape(devices, -1, total.shape[1] // lane, lane).transpose(0, 2, 1, 3)
        out.append(split.reshape(devices, -1, lane))
    return jnp.concatenate(out, axis=1)


def back_kernel(own, first, x_ref, vec_ref, dj_ref, w_in, *refs):
    if own:
        dmid_ref, out_ref, sums_ref, w_ref, arrived = refs
    else:
        out_ref, sums_ref = refs
    D = x_ref.shape[1]
    n = dj_ref.shape[0]
    start = pl.program_id(0) == 0
    copies = [pltpu.make_async_copy(w_in.at[:, i * D:(i + 1) * D], w_ref.at[i], arrived.at[i]) for i in range(n)] if own else []

    @pl.when(start)
    def _():
        for copy in copies:
            copy.start()
        sums_ref[...] = jnp.zeros(sums_ref.shape, f32)

    hat, rstd = ln_parts(x_ref[...].astype(f32) + vec_ref[ROW:ROW + 1, :])
    grad = None
    for i in range(n):
        if own:
            pl.when(start)(copies[i].wait)
            w = w_ref[i]
        else:
            w = w_in[:, first + i * D:first + (i + 1) * D]
        part = dot(dj_ref[i], w, NT)
        grad = part if grad is None else grad + part
    d = ln_back(grad, hat, rstd, vec_ref[GAIN_ONE:GAIN_ONE + 1, :])
    if own:
        d = d + dmid_ref[...]
    out_ref[...] = d.astype(out_ref.dtype)
    sums = [col_sum(d), col_sum(grad * hat), col_sum(grad), col_sum(dj_ref[n - 1])]
    if own:
        sums.append(col_sum(dj_ref[0]))
    for i, p in enumerate(sums):
        sums_ref[i:i + 1, :] += p


def back(x, vectors, dj, w, first, dmid=None, deps=()):
    T, D = x.shape
    n = dj.shape[0]
    own = dmid is not None
    part = pl.BlockSpec((BLOCK, D), lambda i: (i, 0))
    ins = [*in_hbm(x), vectors, *in_vmem(dj), *in_hbm(w, dmid)] if own else [x, vectors, *in_vmem(dj, w)]
    specs = [part, whole(*vectors.shape), pl.BlockSpec((n, BLOCK, D), lambda i: (0, i, 0)),
             pl.BlockSpec(memory_space=pltpu.HBM) if own else whole(*w.shape)]
    return call(
        functools.partial(back_kernel, own, first), (T // BLOCK,), specs + ([part] if own else []), [part, held(8, D)],
        [far((T, D), f32 if own else bf16), shape((8, D), f32)],
        2 * T * D * n * D * 1.5, 16e6, [pltpu.VMEM((n, D, D), bf16), pltpu.SemaphoreType.DMA((n,))] if own else [], deps=deps, mib=M_BACK if own else M_BACKE,
    )(*ins)


class Scatter:
    def __init__(self, mesh, x_first):
        self.seq, self.dp = mesh.shape["seq"], mesh.shape["dp"]
        bits = []
        step = 2
        while step < self.dp:
            bits.append(step)
            step *= 2
        if x_first:
            self.orders = [[0] + bits, bits + [0]]
        else:
            self.orders = [bits + [0], [bits[1], bits[0], 0] + bits[2:]]
        self.stages = len(bits) + 1
        self.count = 1 << self.stages

    def block(self, core, place):
        s, d = 0, core
        for k, bit in enumerate(self.orders[core]):
            on = (place >> (self.stages - 1 - k)) & 1
            if bit == 0:
                s = on
            else:
                d += bit * on
        return s * self.dp + d

    def places(self):
        table = [[0] * self.count for _ in range(2)]
        for c in range(2):
            for p in range(self.count):
                table[c][self.block(c, p) // 2] = p
        return jnp.array(table, jnp.int32)

    def mine_theirs(self, grad):
        core = lax.axis_index("dp") % 2
        pick = [grad[jnp.array([self.block(c, p) for p in range(self.count)])] for c in range(2)]
        return jnp.where(core == 0, pick[0], pick[1]), jnp.where(core == 0, pick[1], pick[0])

    def begin(self, mine, theirs):
        got = lax.ppermute(theirs, "dp", [(i, i ^ 1) for i in range(self.dp)])
        return [mine, got], [0, 0], self.count

    def pairs(self, k):
        pairs = []
        for a in range(self.seq):
            for b in range(self.dp):
                bit = self.orders[b % 2][k]
                to = ((1 - a) * self.dp + b) if bit == 0 else (a * self.dp + (b ^ bit))
                pairs.append((a * self.dp + b, to))
        return pairs

    def total(self, state, at, size):
        arrays, bases, _ = state
        return sum(lax.dynamic_slice_in_dim(a, base + at, size, 0).astype(f32) for a, base in zip(arrays, bases))

    def step(self, k, state, beside=None):
        d = lax.axis_index("dp")
        core = d % 2
        own = [lax.axis_index("seq") if o[k] == 0 else (d // o[k]) % 2 for o in self.orders]
        own = jnp.where(core == 0, own[0], own[1])
        arrays, bases, size = state
        half = size // 2
        send = self.total(state, (1 - own) * half, half).astype(bf16)
        if beside is not None:
            send, *beside = lax.optimization_barrier((send, *beside))
        got = lax.ppermute(send, ("seq", "dp"), self.pairs(k))
        return (arrays + [got], [base + own * half for base in bases] + [0], half), send if beside is None else beside

    def finish(self, first, state):
        for k in range(first, self.stages):
            state, _ = self.step(k, state)
        return self.total(state, 0, 1)[0]


def tie(state, *others):
    arrays, bases, size = state
    out = lax.optimization_barrier(tuple(arrays) + others)
    return (list(out[:len(arrays)]), bases, size), out[len(arrays):]


def make_local(mesh):
    scatter, scatter_b = Scatter(mesh, False), Scatter(mesh, True)
    devices = scatter.seq * scatter.dp

    def local(tokens, domain, domain_table, gain_one, shift_one, wqkv, bias_q, bias_v, w_out, b_out,
              gain_two, shift_two, w_up, b_up, w_down, b_down, cotangent):
        _, T, D = tokens.shape
        F = w_up.shape[1]
        share, ff = D // devices, F // devices
        kernels = share % 16 == 0
        line = [domain_table[domain[0]], gain_one, shift_one, bias_q, None, bias_v, b_out, gain_two, shift_two, b_down]
        line += [b_up[i:i + D] for i in range(0, F, D)]
        at = lax.broadcasted_iota(jnp.int32, (16, D), 0)
        vectors = jnp.zeros((16, D), f32)
        for i, v in enumerate(line):
            if v is not None:
                vectors = jnp.where(at == i, v.astype(f32)[None, :], vectors)
        pos = lax.axis_index("seq").astype(jnp.int32)[None]
        core = (lax.axis_index("dp") % 2).astype(jnp.int32)[None]
        place, place_b = scatter.places(), scatter_b.places()
        x, g = tokens[0], cotangent[0]
        early_x = lax.ppermute(x, "seq", [(0, 1)])

        normed, joined = project(x, vectors, wqkv, 0)
        o1, lse1 = own_forward(joined, D)
        d_act = times(g, w_down)
        normed_e, joined_e = project(early_x, vectors, wqkv, D, [d_act, o1])
        attended, rest, lse = early_forward(pos, joined, joined_e, o1, lse1)
        output, d_mid, d_att, branch, n2, active, g_upper, delta, sums_two, bup_sum = ffn(
            x, attended, rest, vectors, g, d_act, w_out, w_up, w_down)
        if kernels:
            parts = [([(0, 0, None)], ff, 0), ([(1, 1, None)], share, ff), ([(2, 2, None)], share, ff + 2 * share)]
            a = grads(core, place, [active, n2, attended], [g, g_upper, branch], parts, devices)
        else:
            a = scatter.mine_theirs(jnp.concatenate([
                plain_grads([active], [[(0, g, 0)]], devices),
                plain_grads([n2], [[(0, g_upper, 0)]], devices),
                plain_grads([attended], [[(0, branch, 0)]], devices)], axis=1))
        a = scatter.begin(*a)
        dq_e, dj_e, token = early_backward(pos, joined, joined_e, d_att, delta, lse)
        a, (token,) = tie(a, token)
        a, sent = scatter.step(0, a)
        dln_e, sums_e = back(early_x, vectors, dj_e, wqkv, D, None, [sent, token])
        from_late = lax.ppermute(dln_e, "seq", [(1, 0)])
        dj, token = own_backward(pos, joined, d_att, delta, lse, dq_e, [dln_e])
        a, (token,) = tie(a, token)
        a, sent = scatter.step(1, a)
        terms = [[(0, dj, 0)], [(0, dj, 1), (1, dj_e, 0)], [(0, dj, 2), (1, dj_e, 1)]]
        if kernels:
            parts = [([(0, 0, 0)], share, 0), ([(0, 0, 1), (1, 1, 0)], share, share), ([(0, 0, 2), (1, 1, 1)], share, 2 * share)]
            b = grads(core, place_b, in_hbm(normed, normed_e), [dj, dj_e], parts, devices, [sent, token])
        else:
            b = scatter_b.mine_theirs(plain_grads([normed, normed_e], terms, devices))
        a, (from_late, *b) = tie(a, from_late, *b)
        a, (theirs,) = scatter.step(2, a, [b[1]])
        b = scatter_b.begin(b[0], theirs)
        b, sent = scatter_b.step(0, b)
        base, sums_one = back(x, vectors, dj, wqkv, 0, d_mid, [sent])
        b, (base,) = tie(b, base)
        sums_one = jnp.concatenate([sums_one[:4] + sums_e[:4], sums_one[4:5]], axis=0)
        domains = domain_table.shape[0]
        onehot = (jnp.arange(domains, dtype=jnp.int32) == domain[0]).astype(f32)
        small = jnp.concatenate([
            onehot[:, None] * sums_one[:1], sums_one[1:3], sums_one[4:5], sums_one[3:4], sums_two[:4]], axis=0)
        small = small.reshape(-1, devices, share).transpose(1, 0, 2).reshape(devices, -1)
        small = jnp.concatenate([small, bup_sum.reshape(devices, -1)], axis=1)
        b, (small,) = scatter_b.step(1, b, [small])
        a, (base,) = tie(a, base)
        a, _ = scatter.step(3, a)
        flat = jnp.sum(lax.all_to_all(small, ("seq", "dp"), 0, 0, tiled=True), axis=0)
        b, (flat,) = scatter_b.step(2, b, [flat])
        a, (flat,) = tie(a, flat)
        grad_tokens = (base + from_late.astype(f32)).astype(bf16)
        b, (grad_tokens,) = tie(b, grad_tokens)
        sum_b = scatter_b.finish(3, b)
        sum_a = scatter.finish(4, a)

        join = lambda a, n: jnp.concatenate([a[i * share:(i + 1) * share] for i in range(n)], axis=1)
        piece = lambda i: flat[i * share:(i + 1) * share]
        m = domains
        return (
            output[None], grad_tokens[None], flat[:m * share].reshape(m, share), piece(m), piece(m + 1), join(sum_b, 3),
            piece(m + 2), piece(m + 3), sum_a[ff + 2 * share:], piece(m + 4), piece(m + 5), piece(m + 6),
            join(sum_a[ff:], 2), flat[(m + 8) * share:(m + 8) * share + ff], sum_a[:ff], piece(m + 7))

    return local


def solution(mesh):
    both = ("seq", "dp")
    lead, rows = P("dp", "seq", None), P(both, None)
    return jax.shard_map(
        make_local(mesh),
        mesh=mesh,
        in_specs=(lead, P("dp")) + (P(),) * 14 + (lead,),
        out_specs=(lead, lead, P(None, both), P(both), P(both), rows, P(both), P(both), rows, P(both), P(both), P(both),
                   rows, P(both), rows, P(both)),
        check_vma=False,
    )
```

```python
import functools

import jax
import jax.numpy as jnp
from jax import lax
from jax.experimental import pallas as pl
from jax.experimental.pallas import tpu as pltpu
from jax.sharding import PartitionSpec as P

HEAD_DIM = 128
EPSILON = 1e-05
LOG2E = 1.4426950408889634
BLOCK = 256
COST = 0.05
MIB_FFN = 22
M_PROJ, M_OWN, M_EARLY, M_BWD, M_TIMES, M_BACK, M_BACKE, M_GRADS = 14, 16, 16, 30, 14, 24, 16, 18
f32, bf16 = jnp.float32, jnp.bfloat16
NN = ((1,), (0,))
NT = ((1,), (1,))
TN = ((0,), (0,))
ROW, GAIN_ONE, SHIFT_ONE, BIAS, B_OUT, GAIN_TWO, SHIFT_TWO, B_DOWN, B_UP = 0, 1, 2, 3, 6, 7, 8, 9, 10
SMEM = pl.BlockSpec(memory_space=pltpu.SMEM)


def dot(a, b, dims):
    return lax.dot_general(a, b, (dims, ((), ())), preferred_element_type=f32)


def ignoring(kernel, first, count):
    return lambda *refs: kernel(*refs[:first], *refs[first + count:])


def call(kernel, grid, in_specs, out_specs, out_shape, flops, moved, scratch=(), mib=20, aliases=None, deps=()):
    n = len(in_specs)
    run = pl.pallas_call(
        ignoring(kernel, n, len(deps)),
        grid=grid,
        in_specs=list(in_specs) + [pl.BlockSpec(memory_space=pl.ANY)] * len(deps),
        out_specs=out_specs,
        out_shape=out_shape,
        scratch_shapes=list(scratch),
        input_output_aliases=aliases or {},
        cost_estimate=pl.CostEstimate(flops=int(flops * COST), bytes_accessed=int(moved * COST), transcendentals=0),
        compiler_params=pltpu.CompilerParams(vmem_limit_bytes=mib * 2**20),
    )
    return lambda *args: run(*args, *deps)


def shape(dims, kind):
    return jax.ShapeDtypeStruct(dims, kind)


def near(dims, kind):
    return pltpu.VMEM(dims, kind)


def far(dims, kind):
    return pltpu.HBM(dims, kind)


def in_vmem(*arrays):
    return [pltpu.with_memory_space_constraint(a, pltpu.VMEM) for a in arrays]


def in_hbm(*arrays):
    return [pltpu.with_memory_space_constraint(a, pltpu.HBM) for a in arrays]


def whole(*dims):
    return pl.BlockSpec(dims, lambda *_: (0,) * len(dims), pipeline_mode=pl.Buffered(1))


def held(*dims):
    return pl.BlockSpec(dims, lambda *_: (0,) * len(dims))


def ln_parts(x):
    center = x - jnp.mean(x, axis=-1, keepdims=True)
    rstd = lax.rsqrt(jnp.mean(center * center, axis=-1, keepdims=True) + EPSILON)
    return center * rstd, rstd


def ln_back(grad, hat, rstd, gain):
    g = grad * gain
    return rstd * (g - jnp.mean(g, axis=-1, keepdims=True) - hat * jnp.mean(g * hat, axis=-1, keepdims=True))


def col_sum(a):
    return jnp.sum(a.astype(f32), axis=0, keepdims=True)


def project_kernel(first, x_ref, vec_ref, w_ref, normed_ref, out_ref):
    @pl.when(pl.program_id(0) == 0)
    def _():
        for i in range(x_ref.shape[0] // BLOCK):
            rows = slice(i * BLOCK, (i + 1) * BLOCK)
            hat, _ = ln_parts(x_ref[rows, :].astype(f32) + vec_ref[ROW:ROW + 1, :])
            normed_ref[rows, :] = (hat * vec_ref[GAIN_ONE:GAIN_ONE + 1, :] + vec_ref[SHIFT_ONE:SHIFT_ONE + 1, :]).astype(bf16)

    wide = w_ref.shape[1]
    at = first + pl.program_id(0) * wide
    lane = x_ref.shape[1]
    bias = vec_ref[pl.ds(BIAS + at // lane, 1), pl.ds(pl.multiple_of(at % lane, wide), wide)]
    out_ref[...] = (dot(normed_ref[...], w_ref[...], NN) + bias).astype(bf16)


def project(x, vectors, w, first, deps=()):
    T, D = x.shape
    wide = 512
    steps = (w.shape[1] - first) // wide
    skip = first // wide
    return call(
        functools.partial(project_kernel, first), (steps,),
        [whole(T, D), whole(*vectors.shape), pl.BlockSpec((D, wide), lambda c: (0, c + skip))],
        [held(T, D), pl.BlockSpec((T, wide), lambda c: (0, c))],
        [far((T, D), bf16), near((T, steps * wide), bf16)],
        2 * T * D * wide * steps, 10e6, deps=deps, mib=M_PROJ,
    )(x, vectors, *in_hbm(w))


def columns(first, h):
    if isinstance(h, int):
        return slice(first + h * HEAD_DIM, first + (h + 1) * HEAD_DIM)
    return pl.ds(pl.multiple_of(first + h * HEAD_DIM, HEAD_DIM), HEAD_DIM)


def own_forward_kernel(j_ref, o_ref, lse_ref):
    T, D = o_ref.shape
    c = HEAD_DIM ** -0.5 * LOG2E
    row = lax.broadcasted_iota(jnp.int32, (BLOCK, BLOCK), 0)
    col = lax.broadcasted_iota(jnp.int32, (BLOCK, BLOCK), 1)
    for pair in range(2):
        h = pl.program_id(0) * 2 + pair
        head, k_head, v_head = (columns(i * D, h) for i in range(3))
        for i in range(T // BLOCK):
            rows = slice(i * BLOCK, (i + 1) * BLOCK)
            q = j_ref[rows, head]
            last = jnp.where(col <= row, dot(q, j_ref[rows, k_head], NT), -1e30)
            top = jnp.max(last, axis=1, keepdims=True)
            if i:
                s = dot(q, j_ref[:i * BLOCK, k_head], NT)
                top = jnp.maximum(top, jnp.max(s, axis=1, keepdims=True))
            top = top * c
            p = jnp.exp2(last * c - top)
            total = jnp.sum(p, axis=1, keepdims=True)
            o = dot(p.astype(bf16), j_ref[rows, v_head], NN)
            if i:
                p = jnp.exp2(s * c - top)
                total += jnp.sum(p, axis=1, keepdims=True)
                o += dot(p.astype(bf16), j_ref[:i * BLOCK, v_head], NN)
            o_ref[rows, head] = o / total
            lse_ref[rows, head] = jnp.broadcast_to(top + jnp.log2(total), (BLOCK, HEAD_DIM))


def early_forward_kernel(pos_ref, j_ref, e_ref, o1_ref, lse1_ref, att_ref, rest_ref, row_ref):
    T, D = att_ref.shape
    c = HEAD_DIM ** -0.5 * LOG2E
    shut = jnp.where(pos_ref[0] > 0, 0.0, -1e30).astype(f32)
    units = [(i, pl.program_id(0) * 2 + pair) for pair in range(2) for i in range(T // BLOCK)]

    def scores(i, h):
        return dot(j_ref[i * BLOCK:(i + 1) * BLOCK, columns(0, h)], e_ref[:, columns(0, h)], NT)

    ahead = scores(*units[0])
    for n, (i, h) in enumerate(units):
        rows, head = slice(i * BLOCK, (i + 1) * BLOCK), columns(0, h)
        s = ahead
        if n + 1 < len(units):
            ahead = scores(*units[n + 1])
        top = jnp.max(s, axis=1, keepdims=True) * c
        p = jnp.exp2(s * c - top)
        total = jnp.sum(p, axis=1, keepdims=True)
        o2 = dot(p.astype(bf16), e_ref[:, columns(D, h)], NN) / total
        lse2 = jnp.broadcast_to(top + jnp.log2(total) + shut, (BLOCK, HEAD_DIM))
        lse1 = lse1_ref[rows, head]
        high = jnp.maximum(lse1, lse2)
        w1, w2 = jnp.exp2(lse1 - high), jnp.exp2(lse2 - high)
        both = w1 + w2
        o = (o1_ref[rows, head] * w1 + o2 * w2) / both
        low = o.astype(bf16)
        att_ref[rows, head] = low
        rest_ref[rows, head] = (o - low.astype(f32)).astype(bf16)
        row_ref[h, :, rows] = jnp.transpose(high + jnp.log2(both))[:8, :]


def all_of(*arrays):
    return [whole(*a.shape) for a in arrays]


def own_forward(joined, D):
    T = joined.shape[0]
    out = near((T, D), f32)
    return call(
        own_forward_kernel, (D // HEAD_DIM // 2,), all_of(joined), [whole(T, D)] * 2, [out, out], 12e9, 10e6, mib=M_OWN,
    )(*in_vmem(joined))


def early_forward(pos, joined, joined_e, o1, lse1):
    T, D = o1.shape
    H = D // HEAD_DIM
    return call(
        early_forward_kernel, (H // 2,), [SMEM] + all_of(joined, joined_e, o1, lse1), [whole(T, D)] * 2 + [whole(H, 8, T)],
        [near((T, D), bf16), near((T, D), bf16), near((H, 8, T), f32)], 20e9, 12e6, mib=M_EARLY,
    )(pos, *in_vmem(joined, joined_e, o1, lse1))


def backward_kernel(causal, pos_ref, q_ref, k_ref, v_ref, do_ref, delta_ref, lse_ref, *refs):
    if causal:
        dq_in, out_ref, token_ref, dq_acc = refs
    else:
        dq_out, out_ref, token_ref, dq_acc = refs
    T, wide = q_ref.shape
    token_ref[...] = jnp.zeros(token_ref.shape, f32)
    scale = HEAD_DIM ** -0.5
    c = scale * LOG2E
    base = 1 if causal else 0
    key = lax.broadcasted_iota(jnp.int32, (BLOCK, BLOCK), 0)
    qry = lax.broadcasted_iota(jnp.int32, (BLOCK, BLOCK), 1)
    n = T // BLOCK
    many = wide // HEAD_DIM
    for h in range(many):
        head = columns(0, h)
        delta = delta_ref[pl.ds(pl.program_id(0) * many + h, 1), :]
        lse = lse_ref[h, :1, :]
        if not causal:
            lse = lse + jnp.where(pos_ref[0] > 0, 0.0, 1e30).astype(f32)
        for j in range(n):
            rows = slice(j * BLOCK, (j + 1) * BLOCK)
            a = j * BLOCK if causal else 0
            k = k_ref[rows, head]
            q = q_ref[a:, head]
            do = do_ref[a:, head]
            s = dot(k, q, NT)
            p = jnp.exp2(s * c - lse[:, a:])
            if causal:
                first = jnp.where(key <= qry, p[:, :BLOCK], 0.0)
                p = first if j == n - 1 else jnp.concatenate([first, p[:, BLOCK:]], axis=1)
            dp = dot(v_ref[rows, head], do, NT)
            ds = (p * (dp - delta[:, a:])).astype(bf16)
            out_ref[base + 1, rows, head] = dot(p.astype(bf16), do, NN).astype(bf16)
            out_ref[base, rows, head] = (dot(ds, q, NN) * scale).astype(bf16)
            part = jnp.transpose(dot(k, ds, TN))
            if j == 0:
                dq_acc[h] = part
            else:
                dq_acc[h, a:, :] += part
        dq = dq_acc[h] * scale
        if causal:
            out_ref[0, :, head] = (dq + dq_in[:, head]).astype(bf16)
        else:
            dq_out[:, head] = dq


MANY = 4


def backward_specs(T, D):
    H = D // HEAD_DIM
    spec = lambda skip=0: pl.BlockSpec((T, MANY * HEAD_DIM), lambda h: (0, h + skip * H // MANY))
    parts = lambda n: pl.BlockSpec((n, T, MANY * HEAD_DIM), lambda h: (0, 0, h))
    return H // MANY, spec, parts, [whole(H, T), pl.BlockSpec((MANY, 8, T), lambda h: (h, 0, 0))], [pltpu.VMEM((MANY, T, HEAD_DIM), f32)]


def early_backward(pos, joined, joined_e, do, delta, lse):
    T, D = do.shape
    steps, spec, parts, rows, scratch = backward_specs(T, D)
    return call(
        functools.partial(backward_kernel, False), (steps,), [SMEM, spec(), spec(), spec(1), spec()] + rows,
        [spec(), parts(2), held(8, HEAD_DIM)], [far((T, D), f32), near((2, T, D), bf16), shape((8, HEAD_DIM), f32)],
        26e9, 14e6, scratch, mib=M_BWD,
    )(pos, *in_hbm(joined, joined_e, joined_e, do), *in_vmem(delta, lse))


def own_backward(pos, joined, do, delta, lse, dq, deps=()):
    T, D = do.shape
    steps, spec, parts, rows, scratch = backward_specs(T, D)
    return call(
        functools.partial(backward_kernel, True), (steps,), [SMEM, spec(), spec(1), spec(2), spec()] + rows + [spec()],
        [parts(3), held(8, HEAD_DIM)], [near((3, T, D), bf16), shape((8, HEAD_DIM), f32)],
        22e9, 14e6, scratch, deps=deps, mib=M_BWD,
    )(pos, *in_hbm(joined, joined, joined, do), *in_vmem(delta, lse), *in_hbm(dq))


def ffn_kernel(x_ref, att_ref, rest_ref, vec_ref, g_ref, dact_ref, wo_ref, up_ref, down_ref,
               out_ref, dmid_ref, datt_ref, branch_ref, n2_ref, act_ref, gup_ref, delta_ref, sums_ref, bup_sum_ref):
    D, F, H = x_ref.shape[1], up_ref.shape[1], delta_ref.shape[0]

    first = pl.program_id(0) == 0

    @pl.when(first)
    def _():
        sums_ref[...] = jnp.zeros(sums_ref.shape, f32)
        bup_sum_ref[...] = jnp.zeros(bup_sum_ref.shape, f32)

    vec = lambda i: vec_ref[i:i + 1, :]
    m = x_ref[...].astype(f32) + vec(ROW) + (dot(att_ref[...], wo_ref[...], NN) + vec(B_OUT))
    hat, rstd = ln_parts(m)
    n2_ref[...] = (hat * vec(GAIN_TWO) + vec(SHIFT_TWO)).astype(bf16)
    wide = 512
    for f in range(0, F, wide):
        cols = slice(f, f + wide)
        u = dot(n2_ref[...], up_ref[:, cols], NN) + vec(B_UP + f // D)[:, f % D:f % D + wide]
        d_act = dact_ref[:, cols].astype(f32)
        cdf = 0.5 * (1.0 + lax.erf(u * 0.7071067811865476))
        pdf = jnp.exp(-0.5 * u * u) * 0.3989422804014327
        act_ref[:, cols] = (u * cdf).astype(bf16)
        gup = (d_act * (cdf + u * pdf)).astype(bf16)
        gup_ref[:, cols] = gup
        bup_sum_ref[:, cols] += col_sum(gup)
    grad = dot(gup_ref[...], up_ref[...], NT)
    g = g_ref[...].astype(f32)
    d = g + ln_back(grad, hat, rstd, vec(GAIN_TWO))
    dmid_ref[...] = d
    low = d.astype(bf16)
    branch_ref[...] = low
    out_ref[...] = (m + (dot(act_ref[...], down_ref[...], NN) + vec(B_DOWN))).astype(bf16)
    datt = dot(low, wo_ref[...], NT).astype(bf16)
    datt_ref[...] = datt
    prod = datt.astype(f32) * (att_ref[...].astype(f32) + rest_ref[...].astype(f32))
    high = prod.astype(bf16)
    head = lax.broadcasted_iota(jnp.int32, (H, D), 0)
    heads = (lax.broadcasted_iota(jnp.int32, (H, D), 1) // HEAD_DIM == head).astype(bf16)
    delta_ref[...] = dot(heads, high, NT) + dot(heads, (prod - high.astype(f32)).astype(bf16), NT)
    for i, p in enumerate([col_sum(low), col_sum(grad * hat), col_sum(grad), col_sum(g)]):
        sums_ref[i:i + 1, :] += p


def ffn(x, att, rest, vectors, g, dact, wo, w_up, w_down):
    T, D = x.shape
    F = w_up.shape[1]
    H = D // HEAD_DIM
    part = lambda w: pl.BlockSpec((BLOCK, w), lambda i: (i, 0))
    return call(
        ffn_kernel, (T // BLOCK,),
        [part(D), part(D), part(D), whole(*vectors.shape), part(D), part(F), whole(D, D), whole(D, F), whole(F, D)],
        [part(D)] * 5 + [part(F), part(F), pl.BlockSpec((H, BLOCK), lambda i: (0, i)), held(8, D), held(1, F)],
        [far((T, D), bf16), far((T, D), f32), far((T, D), bf16), near((T, D), bf16), near((T, D), bf16),
         near((T, F), bf16), near((T, F), bf16), near((H, T), f32), shape((8, D), f32), shape((1, F), f32)],
        2 * T * D * (2 * D + 4 * F) * 1.5, 30e6,
        mib=MIB_FFN,
    )(x, *in_vmem(att, rest), vectors, g, dact, *in_vmem(wo, w_up, w_down))


def times_kernel(a_ref, b_ref, out_ref):
    out_ref[...] = dot(a_ref[...], b_ref[...], NT).astype(bf16)


def times(a, b):
    T, D = a.shape
    F = b.shape[0]
    wide = 512
    return call(
        times_kernel, (F // wide,), [whole(T, D), pl.BlockSpec((wide, D), lambda f: (f, 0))], pl.BlockSpec((T, wide), lambda f: (0, f)),
        far((T, F), bf16), 2 * T * D * F, 8e6, mib=M_TIMES,
    )(*in_hbm(a, b))


def grads_kernel(parts, lefts, rights, core_ref, place_ref, *refs):
    left, right = refs[:lefts], refs[lefts:lefts + rights]
    mine_ref, theirs_ref, stage, sent = refs[lefts + rights:]
    core = core_ref[0]
    shards, lane = stage.shape[1], stage.shape[3]
    step = pl.program_id(0)

    def copies(at):
        for i in range(shards // 2):
            for n, (out_ref, kind) in enumerate(((mine_ref, core), (theirs_ref, 1 - core))):
                yield pltpu.make_async_copy(
                    stage.at[at % 2, 2 * i + kind], out_ref.at[place_ref[kind, at * (shards // 2) + i]], sent.at[at % 2, 2 * i + n])

    def wait(at):
        for copy in copies(at):
            copy.wait()

    pl.when(step >= 2)(functools.partial(wait, step - 2))
    for terms, rows, base in parts:
        total = None
        for a, b, sub in terms:
            add = dot(left[a][...], right[b][...] if sub is None else right[b][sub], TN)
            total = add if total is None else total + add
        for h in range(total.shape[1] // lane):
            first = base + h * rows
            stage[step % 2, :, first:first + rows, :] = total[:, h * lane:(h + 1) * lane].reshape(shards, rows, lane).astype(bf16)
    for copy in copies(step):
        copy.start()

    @pl.when(step == pl.num_programs(0) - 1)
    def _():
        wait(step - 1)
        wait(step)


def grads(core, place, lefts, rights, parts, devices, deps=()):
    T = lefts[0].shape[0]
    steps, lane = 4, 1024
    shards = devices // steps
    height = sum(rows * rights[terms[0][1]].shape[-1] // lane for terms, rows, _ in parts)
    ins = list(lefts) + in_vmem(*rights)
    out = far((devices // 2, height, lane), bf16)
    flops = sum(2 * T * rows * devices * rights[b].shape[-1] for terms, rows, _ in parts for _, b, _ in terms)
    hbm = pl.BlockSpec(memory_space=pltpu.HBM)
    return call(
        functools.partial(grads_kernel, parts, len(lefts), len(rights)), (steps,),
        [SMEM, SMEM] + [pl.BlockSpec((T, a.shape[1] // steps), lambda s: (0, s)) for a in lefts] + all_of(*rights), [hbm, hbm], [out, out],
        1.5 * flops, 20e6, [pltpu.VMEM((2, shards, height, lane), bf16), pltpu.SemaphoreType.DMA((2, shards))],
        deps=deps, mib=M_GRADS,
    )(core, place, *ins)


def plain_grads(lefts, terms, devices):
    out = []
    for group in terms:
        total = sum(dot(lefts[a], b if b.ndim == 2 else b[p], TN) for a, b, p in group).astype(bf16)
        lane = 1024
        split = total.reshape(devices, -1, total.shape[1] // lane, lane).transpose(0, 2, 1, 3)
        out.append(split.reshape(devices, -1, lane))
    return jnp.concatenate(out, axis=1)


def back_kernel(own, first, x_ref, vec_ref, dj_ref, w_in, *refs):
    if own:
        dmid_ref, out_ref, sums_ref, w_ref, arrived = refs
    else:
        out_ref, sums_ref = refs
    D = x_ref.shape[1]
    n = dj_ref.shape[0]
    start = pl.program_id(0) == 0
    copies = [pltpu.make_async_copy(w_in.at[:, i * D:(i + 1) * D], w_ref.at[i], arrived.at[i]) for i in range(n)] if own else []

    @pl.when(start)
    def _():
        for copy in copies:
            copy.start()
        sums_ref[...] = jnp.zeros(sums_ref.shape, f32)

    hat, rstd = ln_parts(x_ref[...].astype(f32) + vec_ref[ROW:ROW + 1, :])
    grad = None
    for i in range(n):
        if own:
            pl.when(start)(copies[i].wait)
            w = w_ref[i]
        else:
            w = w_in[:, first + i * D:first + (i + 1) * D]
        part = dot(dj_ref[i], w, NT)
        grad = part if grad is None else grad + part
    d = ln_back(grad, hat, rstd, vec_ref[GAIN_ONE:GAIN_ONE + 1, :])
    if own:
        d = d + dmid_ref[...]
    out_ref[...] = d.astype(out_ref.dtype)
    sums = [col_sum(d), col_sum(grad * hat), col_sum(grad), col_sum(dj_ref[n - 1])]
    if own:
        sums.append(col_sum(dj_ref[0]))
    for i, p in enumerate(sums):
        sums_ref[i:i + 1, :] += p


def back(x, vectors, dj, w, first, dmid=None, deps=()):
    T, D = x.shape
    n = dj.shape[0]
    own = dmid is not None
    part = pl.BlockSpec((BLOCK, D), lambda i: (i, 0))
    ins = [*in_hbm(x), vectors, *in_vmem(dj), *in_hbm(w, dmid)] if own else [x, vectors, *in_vmem(dj, w)]
    specs = [part, whole(*vectors.shape), pl.BlockSpec((n, BLOCK, D), lambda i: (0, i, 0)),
             pl.BlockSpec(memory_space=pltpu.HBM) if own else whole(*w.shape)]
    return call(
        functools.partial(back_kernel, own, first), (T // BLOCK,), specs + ([part] if own else []), [part, held(8, D)],
        [far((T, D), f32 if own else bf16), shape((8, D), f32)],
        2 * T * D * n * D * 1.5, 16e6, [pltpu.VMEM((n, D, D), bf16), pltpu.SemaphoreType.DMA((n,))] if own else [], deps=deps, mib=M_BACK if own else M_BACKE,
    )(*ins)


class Scatter:
    def __init__(self, mesh, x_first):
        self.seq, self.dp = mesh.shape["seq"], mesh.shape["dp"]
        bits = []
        step = 2
        while step < self.dp:
            bits.append(step)
            step *= 2
        if x_first:
            self.orders = [[0] + bits, bits + [0]]
        else:
            self.orders = [bits + [0], [bits[1], bits[0], 0] + bits[2:]]
        self.stages = len(bits) + 1
        self.count = 1 << self.stages

    def block(self, core, place):
        s, d = 0, core
        for k, bit in enumerate(self.orders[core]):
            on = (place >> (self.stages - 1 - k)) & 1
            if bit == 0:
                s = on
            else:
                d += bit * on
        return s * self.dp + d

    def places(self):
        table = [[0] * self.count for _ in range(2)]
        for c in range(2):
            for p in range(self.count):
                table[c][self.block(c, p) // 2] = p
        return jnp.array(table, jnp.int32)

    def mine_theirs(self, grad):
        core = lax.axis_index("dp") % 2
        pick = [grad[jnp.array([self.block(c, p) for p in range(self.count)])] for c in range(2)]
        return jnp.where(core == 0, pick[0], pick[1]), jnp.where(core == 0, pick[1], pick[0])

    def begin(self, mine, theirs):
        got = lax.ppermute(theirs, "dp", [(i, i ^ 1) for i in range(self.dp)])
        return [mine, got], [0, 0], self.count

    def pairs(self, k):
        pairs = []
        for a in range(self.seq):
            for b in range(self.dp):
                bit = self.orders[b % 2][k]
                to = ((1 - a) * self.dp + b) if bit == 0 else (a * self.dp + (b ^ bit))
                pairs.append((a * self.dp + b, to))
        return pairs

    def total(self, state, at, size):
        arrays, bases, _ = state
        return sum(lax.dynamic_slice_in_dim(a, base + at, size, 0).astype(f32) for a, base in zip(arrays, bases))

    def step(self, k, state, beside=None):
        d = lax.axis_index("dp")
        core = d % 2
        own = [lax.axis_index("seq") if o[k] == 0 else (d // o[k]) % 2 for o in self.orders]
        own = jnp.where(core == 0, own[0], own[1])
        arrays, bases, size = state
        half = size // 2
        send = self.total(state, (1 - own) * half, half).astype(bf16)
        if beside is not None:
            send, *beside = lax.optimization_barrier((send, *beside))
        got = lax.ppermute(send, ("seq", "dp"), self.pairs(k))
        return (arrays + [got], [base + own * half for base in bases] + [0], half), send if beside is None else beside

    def finish(self, first, state):
        for k in range(first, self.stages):
            state, _ = self.step(k, state)
        return self.total(state, 0, 1)[0]


def tie(state, *others):
    arrays, bases, size = state
    out = lax.optimization_barrier(tuple(arrays) + others)
    return (list(out[:len(arrays)]), bases, size), out[len(arrays):]


def make_local(mesh):
    scatter, scatter_b = Scatter(mesh, False), Scatter(mesh, True)
    devices = scatter.seq * scatter.dp

    def local(tokens, domain, domain_table, gain_one, shift_one, wqkv, bias_q, bias_v, w_out, b_out,
              gain_two, shift_two, w_up, b_up, w_down, b_down, cotangent):
        _, T, D = tokens.shape
        F = w_up.shape[1]
        share, ff = D // devices, F // devices
        kernels = share % 16 == 0
        line = [domain_table[domain[0]], gain_one, shift_one, bias_q, None, bias_v, b_out, gain_two, shift_two, b_down]
        line += [b_up[i:i + D] for i in range(0, F, D)]
        at = lax.broadcasted_iota(jnp.int32, (16, D), 0)
        vectors = jnp.zeros((16, D), f32)
        for i, v in enumerate(line):
            if v is not None:
                vectors = jnp.where(at == i, v.astype(f32)[None, :], vectors)
        pos = lax.axis_index("seq").astype(jnp.int32)[None]
        core = (lax.axis_index("dp") % 2).astype(jnp.int32)[None]
        place, place_b = scatter.places(), scatter_b.places()
        x, g = tokens[0], cotangent[0]
        early_x = lax.ppermute(x, "seq", [(0, 1)])

        normed, joined = project(x, vectors, wqkv, 0)
        o1, lse1 = own_forward(joined, D)
        d_act = times(g, w_down)
        normed_e, joined_e = project(early_x, vectors, wqkv, D, [d_act, o1])
        attended, rest, lse = early_forward(pos, joined, joined_e, o1, lse1)
        output, d_mid, d_att, branch, n2, active, g_upper, delta, sums_two, bup_sum = ffn(
            x, attended, rest, vectors, g, d_act, w_out, w_up, w_down)
        if kernels:
            parts = [([(0, 0, None)], ff, 0), ([(1, 1, None)], share, ff), ([(2, 2, None)], share, ff + 2 * share)]
            a = grads(core, place, [active, n2, attended], [g, g_upper, branch], parts, devices)
        else:
            a = scatter.mine_theirs(jnp.concatenate([
                plain_grads([active], [[(0, g, 0)]], devices),
                plain_grads([n2], [[(0, g_upper, 0)]], devices),
                plain_grads([attended], [[(0, branch, 0)]], devices)], axis=1))
        a = scatter.begin(*a)
        dq_e, dj_e, token = early_backward(pos, joined, joined_e, d_att, delta, lse)
        a, (token,) = tie(a, token)
        a, sent = scatter.step(0, a)
        dln_e, sums_e = back(early_x, vectors, dj_e, wqkv, D, None, [sent, token])
        from_late = lax.ppermute(dln_e, "seq", [(1, 0)])
        dj, token = own_backward(pos, joined, d_att, delta, lse, dq_e, [dln_e])
        a, (token,) = tie(a, token)
        a, sent = scatter.step(1, a)
        terms = [[(0, dj, 0)], [(0, dj, 1), (1, dj_e, 0)], [(0, dj, 2), (1, dj_e, 1)]]
        if kernels:
            parts = [([(0, 0, 0)], share, 0), ([(0, 0, 1), (1, 1, 0)], share, share), ([(0, 0, 2), (1, 1, 1)], share, 2 * share)]
            b = grads(core, place_b, in_hbm(normed, normed_e), [dj, dj_e], parts, devices, [sent, token])
        else:
            b = scatter_b.mine_theirs(plain_grads([normed, normed_e], terms, devices))
        a, (from_late, *b) = tie(a, from_late, *b)
        a, (theirs,) = scatter.step(2, a, [b[1]])
        b = scatter_b.begin(b[0], theirs)
        b, sent = scatter_b.step(0, b)
        base, sums_one = back(x, vectors, dj, wqkv, 0, d_mid, [sent])
        b, (base,) = tie(b, base)
        sums_one = jnp.concatenate([sums_one[:4] + sums_e[:4], sums_one[4:5]], axis=0)
        domains = domain_table.shape[0]
        onehot = (jnp.arange(domains, dtype=jnp.int32) == domain[0]).astype(f32)
        small = jnp.concatenate([
            onehot[:, None] * sums_one[:1], sums_one[1:3], sums_one[4:5], sums_one[3:4], sums_two[:4]], axis=0)
        small = small.reshape(-1, devices, share).transpose(1, 0, 2).reshape(devices, -1)
        small = jnp.concatenate([small, bup_sum.reshape(devices, -1)], axis=1)
        b, (small,) = scatter_b.step(1, b, [small])
        a, (base,) = tie(a, base)
        a, _ = scatter.step(3, a)
        flat = jnp.sum(lax.all_to_all(small, ("seq", "dp"), 0, 0, tiled=True), axis=0)
        b, (flat,) = scatter_b.step(2, b, [flat])
        a, (flat,) = tie(a, flat)
        grad_tokens = (base + from_late.astype(f32)).astype(bf16)
        b, (grad_tokens,) = tie(b, grad_tokens)
        sum_b = scatter_b.finish(3, b)
        sum_a = scatter.finish(4, a)

        join = lambda a, n: jnp.concatenate([a[i * share:(i + 1) * share] for i in range(n)], axis=1)
        piece = lambda i: flat[i * share:(i + 1) * share]
        m = domains
        return (
            output[None], grad_tokens[None], flat[:m * share].reshape(m, share), piece(m), piece(m + 1), join(sum_b, 3),
            piece(m + 2), piece(m + 3), sum_a[ff + 2 * share:], piece(m + 4), piece(m + 5), piece(m + 6),
            join(sum_a[ff:], 2), flat[(m + 8) * share:(m + 8) * share + ff], sum_a[:ff], piece(m + 7))

    return local


def solution(mesh):
    both = ("seq", "dp")
    lead, rows = P("dp", "seq", None), P(both, None)
    return jax.shard_map(
        make_local(mesh),
        mesh=mesh,
        in_specs=(lead, P("dp")) + (P(),) * 14 + (lead,),
        out_specs=(lead, lead, P(None, both), P(both), P(both), rows, P(both), P(both), rows, P(both), P(both), P(both),
                   rows, P(both), rows, P(both)),
        check_vma=False,
    )
```
